1024 devices in a mesh: row: 64 (over y, x), rep: 16 (over z, core).
Axes of the slice: x: 8, y: 8, z: 8, core: 2. Of those that a mesh axis runs over, the one named last changes fastest.
Arguments:
- features: bfloat16 [32768, 256], P('row'), may hold values from -6 to 6
- w_self: bfloat16 [256, 256], replicated, may hold values from -0.375 to 0.375
- w_neigh: bfloat16 [256, 256], replicated, may hold values from -0.375 to 0.375
- bias_vector: float32 [256], replicated, may hold values from -3 to 3
- cotangent: bfloat16 [32768, 256], P('row'), may hold values from -6 to 6
- adj_values: bfloat16 [64, 16, 64, 128, 128], P('row', 'rep'), may hold values from 0 to 1.25, as said below
- src_slots: int32 [64, 16, 64], P('row', 'rep'), may hold values from 0 to 15, as said below
- dst_slots: int32 [64, 16, 64], P('row', 'rep'), may hold values from 0 to 3
- slot_counts: int32 [64, 16], P('row', 'rep'), may hold values from 0 to 64, as said below
Outputs:
- activations: bfloat16 [32768, 256], P(('row', 'rep'))
- grad_features: bfloat16 [32768, 256], P(('row', 'rep'))
- grad_self: float32 [256, 256], replicated
- grad_neigh: float32 [256, 256], replicated
- grad_bias: float32 [256], replicated
The draws below stay inside these ranges and needn't reach their ends.
Inputs may be any that keep to these rules, and one draw needn't show every extreme that they name: `adj_values`: A is symmetric: whenever source tile b appears in a live slot of destination tile a, destination tile b lists source tile a in a live slot with the transposed tile, and a tile whose destination and source coincide is symmetric. Entries are zero or between 0.125 and 1.25. `src_slots`: an entry q names tile q % 4 of row block c * 4 + q // 4, where c is the replica index. `slot_counts`: live slots come first; at most 16 live slots of a row block and replica name one source row block; no pair of destination and source tiles repeats among them; they are ordered by source block, then destination tile, then source tile.
All inputs are finite; a program needn't handle non-finite values.
Results may differ from the reference program's by a relative error of at most 0.015.
Values may be sent and summed in bfloat16 or wider, within the bound.
A program may use at most 32 MiB of HBM per device.

```python
import math
import jax
import jax.numpy as jnp
from jax import lax

F = 256
H = 256
TILE = 128
PAIR_SLOTS = 16
NB = 512
ROW_BLOCKS = 64
REPLICAS = 16
SECTIONS = 4
TILES_BLK = 4
SLOTS = 64
NODES = 32768


def slot_layout(key):
    base_key = jax.random.fold_in(key, 11)
    tiles_total = ROW_BLOCKS * TILES_BLK
    square = TILES_BLK * TILES_BLK
    level = jax.random.randint(jax.random.fold_in(base_key, 1), (ROW_BLOCKS,), 0, 4)
    outer_shape = (ROW_BLOCKS, REPLICAS, SECTIONS)
    owner = jnp.broadcast_to(jnp.arange(ROW_BLOCKS, dtype=jnp.int32)[:, None, None], outer_shape)
    replica = jnp.broadcast_to(jnp.arange(REPLICAS, dtype=jnp.int32)[None, :, None], outer_shape)
    section = jnp.broadcast_to(jnp.arange(SECTIONS, dtype=jnp.int32)[None, None, :], outer_shape)
    source_block = replica * SECTIONS + section
    lower = jnp.minimum(owner, source_block)
    upper = jnp.maximum(owner, source_block)
    block_pair = lower * ROW_BLOCKS + upper
    wanted = jnp.minimum(PAIR_SLOTS, PAIR_SLOTS * (2 + level[lower] + level[upper]) // 8)
    hub = (lower == 0) & (upper >= SECTIONS) & (upper < 2 * SECTIONS)
    wanted = jnp.where(hub, PAIR_SLOTS, wanted)
    rank_key = jax.random.fold_in(base_key, 2)
    ranks = jax.vmap(lambda pair_one: jnp.argsort(jax.random.permutation(jax.random.fold_in(rank_key, pair_one), square)).astype(jnp.int32))(block_pair.reshape(-1)).reshape(outer_shape + (square,))
    dest_tile = jnp.broadcast_to(jnp.arange(TILES_BLK, dtype=jnp.int32)[:, None], (TILES_BLK, TILES_BLK)).reshape(-1)
    source_tile = jnp.broadcast_to(jnp.arange(TILES_BLK, dtype=jnp.int32)[None, :], (TILES_BLK, TILES_BLK)).reshape(-1)
    forward_pos = dest_tile * TILES_BLK + source_tile
    mirror_pos = source_tile * TILES_BLK + dest_tile
    lower_side = (owner < source_block)[..., None]
    position = jnp.where(lower_side, forward_pos[None, None, None, :], mirror_pos[None, None, None, :])
    rank_here = jnp.take_along_axis(ranks, position, axis=-1)
    same_block = (owner == source_block)[..., None]
    on_diagonal = (dest_tile == source_tile) & (dest_tile < PAIR_SLOTS)
    present = jnp.where(same_block, on_diagonal[None, None, None, :], rank_here < wanted[..., None])
    full_shape = (ROW_BLOCKS, REPLICAS, SECTIONS * square)
    present = present.reshape(full_shape)
    dest_full = jnp.broadcast_to(dest_tile[None, None, None, :], outer_shape + (square,)).reshape(full_shape)
    source_full = jnp.broadcast_to(source_tile[None, None, None, :], outer_shape + (square,)).reshape(full_shape)
    section_full = jnp.broadcast_to(section[..., None], outer_shape + (square,)).reshape(full_shape)
    owner_full = jnp.broadcast_to(owner[..., None], outer_shape + (square,)).reshape(full_shape)
    block_full = jnp.broadcast_to(source_block[..., None], outer_shape + (square,)).reshape(full_shape)
    dest_global = owner_full * TILES_BLK + dest_full
    source_global = block_full * TILES_BLK + source_full
    pair_id = jnp.minimum(dest_global, source_global) * tiles_total + jnp.maximum(dest_global, source_global)
    candidate = jnp.broadcast_to(jnp.arange(SECTIONS * square, dtype=jnp.int32)[None, None, :], full_shape)
    sort_keys = jnp.where(present, 0, SECTIONS * square) + candidate
    order = jnp.argsort(sort_keys, axis=-1)[..., :SLOTS]
    counts = jnp.sum(present.astype(jnp.int32), axis=-1)

    def reorder(values):
        return jnp.take_along_axis(values, order, axis=-1)
    return (reorder(section_full * TILES_BLK + source_full), reorder(dest_full), counts, reorder(pair_id), reorder(dest_global > source_global), reorder(dest_global == source_global))


def draw_adj_values(key, part):
    layout = slot_layout(key)
    value_key = jax.random.fold_in(jax.random.fold_in(key, 11), 3)

    def one_tile(pair_one, flipped, diagonal):
        tile_key = jax.random.fold_in(value_key, pair_one)
        matching = jax.random.permutation(jax.random.fold_in(tile_key, 1), TILE)
        scatter_hits = jax.random.randint(jax.random.fold_in(tile_key, 2), (TILE, TILE), 0, TILE) < 3
        column_ids = jnp.arange(TILE, dtype=jnp.int32)
        nonzero = scatter_hits | (matching[:, None] == column_ids[None, :])
        magnitudes = jax.random.uniform(jax.random.fold_in(tile_key, 3), (TILE, TILE), jnp.float32, 0.25, 1.25)
        tile_values = jnp.where(nonzero, magnitudes, 0.0)
        return jnp.where(diagonal, 0.5 * (tile_values + tile_values.T), jnp.where(flipped, tile_values.T, tile_values))

    def one_block(block_args):
        pair_block, flip_block, diag_block = block_args
        tiles_out = jax.vmap(one_tile)(pair_block.reshape(-1), flip_block.reshape(-1), diag_block.reshape(-1))
        return tiles_out.reshape(REPLICAS, SLOTS, TILE, TILE).astype(jnp.bfloat16)
    return lax.map(one_block, (layout[3], layout[4], layout[5]))


def draw_src_slots(key, part):
    return slot_layout(key)[0]


def draw_dst_slots(key, part):
    return slot_layout(key)[1]


def draw_slot_counts(key, part):
    return slot_layout(key)[2]


def levels(own_key, shape, shards, low, top_value):
    def one(dim, blocks):
        draws = jax.random.uniform(jax.random.fold_in(jax.random.fold_in(own_key, 6), dim), (blocks,), jnp.float32, low / len(shards), top_value / len(shards))
        return jnp.repeat(jnp.exp(draws), shape[dim] // blocks).reshape((-1,) + (1,) * (len(shape) - dim - 1))

    loudness = one(*shards[0])
    for cut in shards[1:]:
        loudness = loudness * one(*cut)
    return loudness


def scatter_about(key, dims, spread, most, cuts=(), kind=jnp.bfloat16):
    result = spread * jax.random.normal(key, dims, jnp.float32)
    if cuts:
        result = result * levels(key, dims, cuts, -0.22, 0.18)
    return jnp.clip(result, -most, most).astype(kind)


def setup_inputs(seed: int = 0) -> dict:
    seeds = jax.random.split(jax.random.key(seed), 10)
    features = scatter_about(seeds[0], (NODES, F), 1.0, 6.0, ((0, 64),))
    w_self = scatter_about(seeds[1], (F, H), F ** -0.5, 0.375)
    w_neigh = scatter_about(seeds[2], (F, H), F ** -0.5, 0.375)
    bias_vector = scatter_about(seeds[3], (H,), 0.5, 3.0, (), jnp.float32)
    cotangent = scatter_about(seeds[4], (NODES, H), 1.0, 6.0, ((0, 64),))
    adj_values = draw_adj_values(jax.random.fold_in(seeds[9], 71), 0)
    src_slots = draw_src_slots(jax.random.fold_in(seeds[9], 71), 0)
    dst_slots = draw_dst_slots(jax.random.fold_in(seeds[9], 71), 0)
    slot_counts = draw_slot_counts(jax.random.fold_in(seeds[9], 71), 0)
    return {"features": features, "w_self": w_self, "w_neigh": w_neigh, "bias_vector": bias_vector, "cotangent": cotangent, "adj_values": adj_values, "src_slots": src_slots, "dst_slots": dst_slots, "slot_counts": slot_counts}


def aggregate_raw(adj_values, src_slots, dst_slots, slot_counts, field):
    field_tiles = field.reshape(ROW_BLOCKS * TILES_BLK, TILE, F)
    replica_base = jnp.arange(REPLICAS, dtype=jnp.int32)[:, None] * (SECTIONS * TILES_BLK)
    slot_index = jnp.arange(SLOTS, dtype=jnp.int32)[None, :]
    dest_range = jnp.arange(TILES_BLK, dtype=jnp.int32)

    def one_block(block_no):
        values = adj_values[block_no].astype(field.dtype)
        sources = replica_base + src_slots[block_no]
        gathered = field_tiles[sources]
        products = jnp.einsum('csab,csbf->csaf', values, gathered, precision=lax.Precision.HIGHEST)
        alive = slot_index < slot_counts[block_no][:, None]
        chosen = ((dst_slots[block_no][:, :, None] == dest_range[None, None, :]) & alive[:, :, None]).astype(field.dtype)
        return jnp.einsum('cst,csaf->taf', chosen, products, precision=lax.Precision.HIGHEST).reshape(NB, F)
    blocks_out = lax.map(one_block, jnp.arange(ROW_BLOCKS, dtype=jnp.int32))
    return blocks_out.reshape(NODES, F)

def transpose_raw(adj_values, src_slots, dst_slots, slot_counts, field):
    field_tiles = field.reshape(ROW_BLOCKS, TILES_BLK, TILE, F)
    replica_base = jnp.arange(REPLICAS, dtype=jnp.int32)[:, None] * (SECTIONS * TILES_BLK)
    slot_index = jnp.arange(SLOTS, dtype=jnp.int32)[None, :]
    dest_range = jnp.arange(TILES_BLK, dtype=jnp.int32)

    def one_block(carried, block_no):
        values = adj_values[block_no].astype(field.dtype)
        alive = slot_index < slot_counts[block_no][:, None]
        chosen = ((dst_slots[block_no][:, :, None] == dest_range[None, None, :]) & alive[:, :, None]).astype(field.dtype)
        dest_rows = jnp.einsum('cst,taf->csaf', chosen, field_tiles[block_no], precision=lax.Precision.HIGHEST)
        sent = jnp.einsum('csab,csaf->csbf', values, dest_rows, precision=lax.Precision.HIGHEST)
        sources = (replica_base + src_slots[block_no]).reshape(-1)
        return (carried.at[sources].add(sent.reshape(-1, TILE, F)), None)
    start_value = jnp.zeros((ROW_BLOCKS * TILES_BLK, TILE, F), field.dtype)
    summed, _ = lax.scan(one_block, start_value, jnp.arange(ROW_BLOCKS, dtype=jnp.int32))
    return summed.reshape(NODES, F)

def reference(features, w_self, w_neigh, bias_vector, cotangent, adj_values, src_slots, dst_slots, slot_counts):
    norm_factor = 1.0 / math.sqrt(SLOTS * REPLICAS / TILES_BLK)
    grad_factor = 1.0 / math.sqrt(NODES)
    raw_sum = aggregate_raw(adj_values, src_slots, dst_slots, slot_counts, features.astype(jnp.float32))
    aggregate = (raw_sum * norm_factor).astype(jnp.bfloat16)
    pre_act = jnp.dot(features, w_self, preferred_element_type=jnp.float32) + jnp.dot(aggregate, w_neigh, preferred_element_type=jnp.float32) + bias_vector
    activations = jax.nn.elu(pre_act).astype(jnp.bfloat16)
    grad_pre = (cotangent.astype(jnp.float32) * jnp.exp(jnp.minimum(pre_act, 0.0))).astype(jnp.bfloat16)
    grad_self = jnp.dot(features.T, grad_pre, preferred_element_type=jnp.float32) * grad_factor
    grad_neigh = jnp.dot(aggregate.T, grad_pre, preferred_element_type=jnp.float32) * grad_factor
    grad_bias = lax.optimization_barrier(jnp.sum(grad_pre.astype(jnp.float32), axis=0)) * grad_factor
    message = jnp.dot(grad_pre, w_neigh.T, preferred_element_type=jnp.float32).astype(jnp.bfloat16)
    returned = transpose_raw(adj_values, src_slots, dst_slots, slot_counts, message.astype(jnp.float32))
    self_term = jnp.dot(grad_pre, w_self.T, preferred_element_type=jnp.float32)
    grad_features = (self_term + returned * norm_factor).astype(jnp.bfloat16)
    return (activations, grad_features, grad_self, grad_neigh, grad_bias)
```

```python
import math

import jax
import jax.numpy as jnp
from jax import lax
from jax.experimental import pallas as pl
from jax.experimental.pallas import tpu as pltpu
from jax.sharding import PartitionSpec as P

RING = 8
HALF = 128
CHUNK = 32
TILE = 128
NB = 512
F = 256
MESH = pl.DeviceIdType.MESH
BF = jnp.bfloat16
F32 = jnp.float32


def wrap(value):
    return lax.rem(value, RING)


def dot_first(a, b):
    return lax.dot_general(a, b, (((0,), (0,)), ((), ())), preferred_element_type=F32)


def dot_last(a, b):
    return lax.dot_general(a, b, (((1,), (1,)), ((), ())), preferred_element_type=F32)


def kernel(
    norm_factor, grad_factor,
    feat, w_self, w_neigh, bias, cot, adj, src_slots, dst_slots, counts,
    act_out, gf_out, gs_out, gn_out, gb_out,
    tiles, dense, part, rec_a, rec_b, mid_a, mid_b, rec_a2, rec_b2, agg,
    f_rows, c_rows, g_own, a_own, act_ret, g_ret, gbuf, acc, back, rec_z, b_sib, b_own,
    gp, gp_rec, gx, gx_rec, gy, gz, gfull, gbias,
    tile_sem, s_t, r_t, s_adj, r_adj, s_a1, r_a1, s_b1, r_b1, s_a2, r_a2, s_b2, r_b2,
    s_agg, r_agg, s_ga1, r_ga1, s_gb1, r_gb1, s_ga2, r_ga2, s_gb2, r_gb2, s_ret, r_ret,
    s_gz, r_gz, s_gx, r_gx, s_gy, r_gy, s_hx, r_hx, s_hz, r_hz, s_hs, r_hs,
    s_z, r_z, s_sib, r_sib,
):
    row = lax.axis_index("row")
    rep = lax.axis_index("rep")
    y, x = row // RING, lax.rem(row, RING)
    z, k = rep // 2, lax.rem(rep, 2)
    sib = 1 - k

    def at(xx, yy, zz, kk):
        return (yy * RING + xx, zz * 2 + kk)

    def along(axis, d):
        if axis == "x":
            return at(wrap(x + d), y, z, k)
        if axis == "y":
            return at(x, wrap(y + d), z, k)
        return at(x, y, wrap(z + d), k)

    def remote(src, dst, send_sem, recv_sem, device):
        return pltpu.make_async_remote_copy(
            src_ref=src, dst_ref=dst, send_sem=send_sem, recv_sem=recv_sem,
            device_id=device, device_id_type=MESH,
        )

    def peers(fn, first=1):
        def step(d, carry):
            fn(d)
            return carry

        lax.fori_loop(first, RING, step, 0)

    own_chunk = rep
    worker_y = wrap(own_chunk)
    own_half = own_chunk // RING
    is_self = jnp.logical_and(worker_y == y, y == z)

    def worker(core):
        return at(x, worker_y, y, core)

    def owner(half):
        return at(x, z, 4 * half + y // 2, lax.rem(y, 2))

    def owner_is_self(half):
        return jnp.logical_and(is_self, own_half == half)

    barrier = pltpu.get_barrier_semaphore()

    def greet(device):
        pl.semaphore_signal(barrier, inc=1, device_id=device, device_id_type=MESH)

    def greet_peers(d):
        for core in (0, 1):
            greet(at(wrap(x + d), y, z, core))
            greet(at(x, wrap(y + d), z, core))
        greet(at(x, y, wrap(z + d), k))

    peers(greet_peers)
    greet(at(x, y, z, sib))
    for core in (0, 1):
        @pl.when(jnp.logical_not(jnp.logical_and(is_self, k == core)))
        def _():
            greet(worker(core))

        @pl.when(jnp.logical_not(owner_is_self(core)))
        def _():
            greet(owner(core))

    load = pltpu.make_async_copy(adj.at[0, 0], tiles, tile_sem)
    load.start()
    load.wait()
    live = counts[0, 0]

    def build(section, pointer):
        for t in range(4):
            for u in range(4):
                slot = jnp.minimum(pointer, 63)
                hit = jnp.logical_and(
                    pointer < live,
                    jnp.logical_and(
                        src_slots[0, 0, slot] == section * 4 + u, dst_slots[0, 0, slot] == t
                    ),
                )
                tile = tiles[slot]
                dense[4 * k + section, pl.ds(t * TILE, TILE), pl.ds(u * TILE, TILE)] = jnp.where(
                    hit, tile, jnp.zeros_like(tile)
                )
                pointer = pointer + hit.astype(jnp.int32)
        return pointer

    lax.fori_loop(0, 4, build, jnp.int32(0))

    def push(section, carry):
        product = dot_first(dense[4 * k + section], feat[...]).astype(BF)
        part[0, section] = product[:, :HALF]
        part[1, section] = product[:, HALF:]
        return carry

    lax.fori_loop(0, 4, push, 0)

    pl.semaphore_wait(barrier, 40 - 2 * is_self.astype(jnp.int32))

    mine_here = (x // 4) == k

    def a1_copy(section, lane):
        to_x = 4 * k + section
        d = wrap(to_x - x + RING)
        return remote(
            part.at[lane, section, pl.ds(0, 256)], rec_a.at[d],
            s_a1.at[section * 2 + lane], r_a1.at[d], at(to_x, y, z, lane),
        )

    def a1_start(section, carry):
        for lane in (0, 1):
            @pl.when(jnp.logical_not(jnp.logical_and(4 * k + section == x, k == lane)))
            def _():
                a1_copy(section, lane).start()
        return carry

    def b1_copy(d, lane):
        to_y = wrap(y + d)
        return remote(
            part.at[lane, :, pl.ds(256 + CHUNK * to_y, CHUNK)], rec_b.at[d, k],
            s_b1.at[d * 2 + lane], r_b1.at[d * 2 + k], at(x, to_y, z, lane),
        )

    def b1_start(d):
        for lane in (0, 1):
            b1_copy(d, lane).start()

    lax.fori_loop(0, 4, a1_start, 0)
    peers(b1_start)
    b1_copy_sib = remote(
        part.at[sib, :, pl.ds(256 + CHUNK * y, CHUNK)], rec_b.at[0, k],
        s_b1.at[0], r_b1.at[k], at(x, y, z, sib),
    )
    b1_copy_sib.start()
    rec_b[0, k] = part[k, :, pl.ds(pl.multiple_of(256 + CHUNK * y, CHUNK), CHUNK), :]

    @pl.when(mine_here)
    def _():
        rec_a[0] = part[k, x - 4 * k, pl.ds(0, 256), :]

    def t_copies(core):
        rows = pl.ds(CHUNK * own_chunk, CHUNK)
        return (
            remote(feat.at[rows], f_rows.at[own_half], s_t.at[core], r_t.at[own_half], worker(core)),
            remote(
                cot.at[rows, pl.ds(HALF * core, HALF)], c_rows.at[own_half],
                s_t.at[2 + core], r_t.at[2 + own_half], worker(core),
            ),
        )

    for core in (0, 1):
        @pl.when(jnp.logical_not(jnp.logical_and(is_self, k == core)))
        def _():
            for copy in t_copies(core):
                copy.start()

    @pl.when(is_self)
    def _():
        rows = pl.ds(pl.multiple_of(CHUNK * own_chunk, CHUNK), CHUNK)
        f_rows[own_half] = feat[rows, :]
        c_rows[own_half] = cot[rows, pl.ds(pl.multiple_of(HALF * k, HALF), HALF)]

    adj_copy = remote(
        dense.at[pl.ds(4 * k, 4)], dense.at[pl.ds(4 * k, 4)], s_adj.at[0], r_adj.at[0],
        at(x, y, z, sib),
    )
    adj_copy.start()

    for half in (0, 1):
        @pl.when(jnp.logical_not(owner_is_self(half)))
        def _():
            remote(f_rows.at[half], f_rows.at[half], s_t.at[0], r_t.at[half], owner(half)).wait_recv()
            remote(
                c_rows.at[half], c_rows.at[half], s_t.at[2], r_t.at[2 + half], owner(half)
            ).wait_recv()

    lanes = pl.ds(pl.multiple_of(HALF * k, HALF), HALF)
    rows64 = f_rows[...].reshape(64, F)
    self_part = jnp.dot(rows64, w_self[:, lanes], preferred_element_type=F32) + bias[:, lanes]

    def a1_wait(d):
        remote(rec_a.at[d], rec_a.at[d], s_a1.at[0], r_a1.at[d], at(x, y, z, sib)).wait_recv()

    @pl.when(jnp.logical_not(mine_here))
    def _():
        a1_wait(0)

    peers(a1_wait)

    def summed(ref):
        total = ref[0].astype(F32)
        for d in range(1, RING):
            total = total + ref[d].astype(F32)
        return total

    mid_a[...] = summed(rec_a).astype(BF).reshape(RING, CHUNK, HALF)

    def a2_copy(d):
        return remote(
            mid_a.at[wrap(y + d)], rec_a2.at[d], s_a2.at[d], r_a2.at[d], along("y", d)
        )

    peers(lambda d: a2_copy(d).start())
    rec_a2[0] = mid_a[y]

    def b1_wait(d):
        for core in (0, 1):
            remote(
                rec_b.at[d, core], rec_b.at[d, core], s_b1.at[0], r_b1.at[d * 2 + core],
                at(x, y, z, sib),
            ).wait_recv()

    remote(
        rec_b.at[0, sib], rec_b.at[0, sib], s_b1.at[0], r_b1.at[sib], at(x, y, z, sib)
    ).wait_recv()
    peers(b1_wait)
    mid_b[...] = summed(rec_b).astype(BF).reshape(RING, CHUNK, HALF)

    def b2_copy(d):
        return remote(
            mid_b.at[wrap(x + d)], rec_b2.at[d], s_b2.at[d], r_b2.at[d], along("x", d)
        )

    peers(lambda d: b2_copy(d).start())
    rec_b2[0] = mid_b[x]

    peers(lambda d: a2_copy(d).wait_recv())
    agg[k, pl.ds(0, CHUNK), :] = (summed(rec_a2) * norm_factor).astype(BF)
    peers(lambda d: b2_copy(d).wait_recv())
    agg[k, pl.ds(CHUNK, CHUNK), :] = (summed(rec_b2) * norm_factor).astype(BF)
    agg_copy = remote(agg.at[k], agg.at[k], s_agg.at[0], r_agg.at[0], at(x, y, z, sib))
    agg_copy.start()
    remote(agg.at[sib], agg.at[sib], s_agg.at[0], r_agg.at[0], at(x, y, z, sib)).wait_recv()

    pre = (
        self_part
        + jnp.dot(agg[0], w_neigh[pl.ds(0, HALF), lanes], preferred_element_type=F32)
        + jnp.dot(agg[1], w_neigh[pl.ds(HALF, HALF), lanes], preferred_element_type=F32)
    )
    low = jnp.exp(jnp.minimum(pre, 0.0))
    grad = (c_rows[...].reshape(64, HALF).astype(F32) * low).astype(BF)
    g_own[...] = grad.reshape(2, CHUNK, HALF)
    a_own[...] = jnp.where(pre > 0, pre, low - 1.0).astype(BF).reshape(
        2, CHUNK, HALF
    )

    place_a = gbuf.at[x, pl.ds(CHUNK * y, CHUNK)]
    place_b = gbuf.at[x, pl.ds(256 + CHUNK * y, CHUNK)]
    gbuf[x, pl.ds(pl.multiple_of(CHUNK * y, CHUNK), CHUNK), :] = g_own[0]
    gbuf[x, pl.ds(pl.multiple_of(256 + CHUNK * y, CHUNK), CHUNK), :] = g_own[1]

    def ga1_copy(d):
        return remote(g_own.at[0], place_a, s_ga1.at[d], r_ga1.at[d], along("y", d))

    def gb1_copy(d):
        return remote(g_own.at[1], place_b, s_gb1.at[d], r_gb1.at[d], along("x", d))

    def g1_start(d):
        ga1_copy(d).start()
        gb1_copy(d).start()

    peers(g1_start)

    def ret_copies(half):
        return (
            remote(a_own.at[half], act_ret.at[k], s_ret.at[half], r_ret.at[k], owner(half)),
            remote(g_own.at[half], g_ret.at[k], s_ret.at[2 + half], r_ret.at[2 + k], owner(half)),
        )

    for half in (0, 1):
        @pl.when(jnp.logical_not(owner_is_self(half)))
        def _():
            for copy in ret_copies(half):
                copy.start()

    @pl.when(is_self)
    def _():
        act_ret[k] = a_own[own_half]
        g_ret[k] = g_own[own_half]

    grad_s = dot_first(rows64, grad)
    grad_n = jnp.concatenate([dot_first(agg[0], grad), dot_first(agg[1], grad)], 0)
    terms = jnp.concatenate([grad_s, grad_n], 0).reshape(RING, 64, HALF)
    gp[:, pl.ds(0, 64), :] = terms
    col_sum = jnp.broadcast_to(jnp.sum(grad.astype(F32), axis=0, keepdims=True), (8, HALF))
    gp[:, pl.ds(64, 8), :] = jnp.broadcast_to(col_sum[None], (RING, 8, HALF))

    def gz_copy(d):
        return remote(gp.at[wrap(z + d)], gp_rec.at[z], s_gz.at[d], r_gz.at[d], along("z", d))

    peers(lambda d: gz_copy(d).start())
    gp_rec[z] = gp[z]

    def ga2_copy(d):
        whole = gbuf.at[x, pl.ds(0, 256)]
        return remote(whole, whole, s_ga2.at[d], r_ga2.at[d], along("x", d))

    def gb2_copy(d):
        whole = gbuf.at[:, pl.ds(256 + CHUNK * y, CHUNK)]
        return remote(whole, whole, s_gb2.at[d], r_gb2.at[d], along("y", d))

    peers(lambda d: ga1_copy(d).wait_recv())
    peers(lambda d: ga2_copy(d).start())
    peers(lambda d: gb1_copy(d).wait_recv())
    peers(lambda d: gb2_copy(d).start())

    peers(lambda d: gz_copy(d).wait_recv())
    over_z = summed(gp_rec)
    gx[:, pl.ds(0, 8), :] = over_z[:64].reshape(RING, 8, HALF)
    gx[:, pl.ds(8, 8), :] = jnp.broadcast_to(over_z[64:][None], (RING, 8, HALF))

    def gx_copy(d):
        return remote(gx.at[wrap(x + d)], gx_rec.at[x], s_gx.at[d], r_gx.at[d], along("x", d))

    peers(lambda d: gx_copy(d).start())
    gx_rec[x] = gx[x]

    adj_copy.wait_recv()

    def pull(at_x, first):
        acc[...] += jnp.dot(
            dense[at_x, :, pl.ds(first, 256)], gbuf[at_x, pl.ds(first, 256), :],
            preferred_element_type=F32,
        )

    acc[...] = jnp.zeros_like(acc)
    pull(x, 0)

    def pull_a(d):
        from_x = wrap(x - d + RING)
        ga2_copy(d).wait_recv()
        pull(from_x, 0)

    peers(pull_a)

    peers(lambda d: gx_copy(d).wait_recv())
    gy[y] = summed(gx_rec)

    def gy_copy(d):
        return remote(gy.at[y], gy.at[y], s_gy.at[d], r_gy.at[d], along("y", d))

    peers(lambda d: gy_copy(d).start())

    peers(lambda d: gb2_copy(d).wait_recv())
    peers(lambda d: pull(d, 256), 0)
    back[...] = acc[...].astype(BF).reshape(RING, 64, HALF)

    def z_copy(d):
        return remote(back.at[wrap(z + d)], rec_z.at[d], s_z.at[d], r_z.at[d], along("z", d))

    peers(lambda d: z_copy(d).start())
    rec_z[0] = back[z]

    peers(lambda d: gy_copy(d).wait_recv())
    total_y = summed(gy)
    gz[x] = total_y[:8]
    gbias[k] = total_y[8:]

    def hx_copy(d):
        return remote(gz.at[x], gz.at[x], s_hx.at[d], r_hx.at[d], along("x", d))

    peers(lambda d: hx_copy(d).start())
    bias_copy = remote(gbias.at[k], gbias.at[k], s_hs.at[1], r_hs.at[1], at(x, y, z, sib))
    bias_copy.start()

    peers(lambda d: z_copy(d).wait_recv())
    total = summed(rec_z)
    b_own[...] = total.astype(BF).reshape(2, CHUNK, HALF)
    sib_copy = remote(b_own.at[sib], b_sib, s_sib.at[0], r_sib.at[0], at(x, y, z, sib))
    sib_copy.start()

    peers(lambda d: hx_copy(d).wait_recv())
    gfull[k, z] = gz[...].reshape(64, HALF)

    def hz_copy(d):
        return remote(gfull.at[k, z], gfull.at[k, z], s_hz.at[d], r_hz.at[d], along("z", d))

    peers(lambda d: hz_copy(d).start())

    for core in (0, 1):
        @pl.when(jnp.logical_not(jnp.logical_and(is_self, k == core)))
        def _():
            remote(
                act_ret.at[core], act_ret.at[core], s_ret.at[0], r_ret.at[core], worker(core)
            ).wait_recv()
            remote(
                g_ret.at[core], g_ret.at[core], s_ret.at[2], r_ret.at[2 + core], worker(core)
            ).wait_recv()

    act_out[:, pl.ds(0, HALF)] = act_ret[0]
    act_out[:, pl.ds(HALF, HALF)] = act_ret[1]
    own_part = dot_last(g_ret[0], w_self[:, pl.ds(0, HALF)]) + dot_last(
        g_ret[1], w_self[:, pl.ds(HALF, HALF)]
    )
    sib_copy.wait_recv()
    returned = dot_last(b_own[k], w_neigh[:, lanes]) + dot_last(
        b_sib[...], w_neigh[:, pl.ds(pl.multiple_of(HALF * sib, HALF), HALF)]
    )
    gf_out[...] = (own_part + returned * norm_factor).astype(BF)

    peers(lambda d: hz_copy(d).wait_recv())
    full_copy = remote(gfull.at[k], gfull.at[k], s_hs.at[0], r_hs.at[0], at(x, y, z, sib))
    full_copy.start()
    bias_copy.wait_recv()
    for core in (0, 1):
        gb_out[:, pl.ds(HALF * core, HALF)] = gbias[core, pl.ds(0, 1), :] * grad_factor
    remote(
        gfull.at[sib], gfull.at[sib], s_hs.at[0], r_hs.at[0], at(x, y, z, sib)
    ).wait_recv()
    for core in (0, 1):
        gs_out[:, pl.ds(HALF * core, HALF)] = (
            gfull[core, pl.ds(0, 4)].reshape(F, HALF) * grad_factor
        )
        gn_out[:, pl.ds(HALF * core, HALF)] = (
            gfull[core, pl.ds(4, 4)].reshape(F, HALF) * grad_factor
        )

    def a1_done(section, carry):
        for lane in (0, 1):
            @pl.when(jnp.logical_not(jnp.logical_and(4 * k + section == x, k == lane)))
            def _():
                a1_copy(section, lane).wait_send()
        return carry

    lax.fori_loop(0, 4, a1_done, 0)

    def sends_done(d):
        for lane in (0, 1):
            b1_copy(d, lane).wait_send()
        for copy in (
            a2_copy, b2_copy, ga1_copy, gb1_copy, ga2_copy, gb2_copy, gz_copy, gx_copy, gy_copy,
            hx_copy, hz_copy, z_copy,
        ):
            copy(d).wait_send()

    peers(sends_done)
    for copy in (b1_copy_sib, adj_copy, agg_copy, sib_copy, bias_copy, full_copy):
        copy.wait_send()
    for core in (0, 1):
        @pl.when(jnp.logical_not(jnp.logical_and(is_self, k == core)))
        def _():
            for copy in t_copies(core):
                copy.wait_send()

        @pl.when(jnp.logical_not(owner_is_self(core)))
        def _():
            for copy in ret_copies(core):
                copy.wait_send()


def shards(
    features, w_self, w_neigh, bias_vector, cotangent, adj_values, src_slots, dst_slots, slot_counts
):
    block_rows = features.shape[0]
    replicas = lax.axis_size("rep")
    node_total = block_rows * lax.axis_size("row")
    slot_total = adj_values.shape[2]
    norm_factor = 1.0 / math.sqrt(slot_total * replicas / (block_rows // adj_values.shape[-1]))
    grad_factor = 1.0 / math.sqrt(node_total)

    def body(*refs):
        kernel(norm_factor, grad_factor, *refs)

    vmem = pl.BlockSpec(memory_space=pltpu.VMEM)
    smem = pl.BlockSpec(memory_space=pltpu.SMEM)
    dma = pltpu.SemaphoreType.DMA
    sems = [
        dma(()), dma((4,)), dma((4,)), dma((1,)), dma((1,)), dma((8,)), dma((8,)), dma((16,)),
        dma((16,)), dma((8,)), dma((8,)), dma((8,)), dma((8,)),
        dma((1,)), dma((1,)), dma((8,)), dma((8,)), dma((8,)), dma((8,)), dma((8,)), dma((8,)),
        dma((8,)), dma((8,)), dma((4,)), dma((4,)),
        dma((8,)), dma((8,)), dma((8,)), dma((8,)), dma((8,)), dma((8,)), dma((8,)), dma((8,)),
        dma((8,)), dma((8,)), dma((2,)), dma((2,)),
        dma((8,)), dma((8,)), dma((1,)), dma((1,)),
    ]
    scratch = [
        pltpu.VMEM((64, TILE, TILE), BF),
        pltpu.VMEM((8, NB, NB), BF),
        pltpu.VMEM((2, 4, NB, HALF), BF),
        pltpu.VMEM((8, 256, HALF), BF),
        pltpu.VMEM((8, 2, 4, CHUNK, HALF), BF),
        pltpu.VMEM((8, CHUNK, HALF), BF),
        pltpu.VMEM((8, CHUNK, HALF), BF),
        pltpu.VMEM((8, CHUNK, HALF), BF),
        pltpu.VMEM((8, CHUNK, HALF), BF),
        pltpu.VMEM((2, 64, HALF), BF),
        pltpu.VMEM((2, CHUNK, F), BF),
        pltpu.VMEM((2, CHUNK, HALF), BF),
        pltpu.VMEM((2, CHUNK, HALF), BF),
        pltpu.VMEM((2, CHUNK, HALF), BF),
        pltpu.VMEM((2, CHUNK, HALF), BF),
        pltpu.VMEM((2, CHUNK, HALF), BF),
        pltpu.VMEM((8, NB, HALF), BF),
        pltpu.VMEM((NB, HALF), F32),
        pltpu.VMEM((8, 64, HALF), BF),
        pltpu.VMEM((8, 64, HALF), BF),
        pltpu.VMEM((CHUNK, HALF), BF),
        pltpu.VMEM((2, CHUNK, HALF), BF),
        pltpu.VMEM((8, 72, HALF), F32),
        pltpu.VMEM((8, 72, HALF), F32),
        pltpu.VMEM((8, 16, HALF), F32),
        pltpu.VMEM((8, 16, HALF), F32),
        pltpu.VMEM((8, 16, HALF), F32),
        pltpu.VMEM((8, 8, HALF), F32),
        pltpu.VMEM((2, 8, 64, HALF), F32),
        pltpu.VMEM((2, 8, HALF), F32),
    ]
    outs = pl.pallas_call(
        body,
        out_shape=(
            jax.ShapeDtypeStruct((CHUNK, F), BF),
            jax.ShapeDtypeStruct((CHUNK, F), BF),
            jax.ShapeDtypeStruct((F, F), F32),
            jax.ShapeDtypeStruct((F, F), F32),
            jax.ShapeDtypeStruct((1, F), F32),
        ),
        in_specs=[vmem] * 5 + [pl.BlockSpec(memory_space=pl.ANY)] + [smem] * 3,
        out_specs=(vmem,) * 5,
        scratch_shapes=scratch + sems,
        compiler_params=pltpu.CompilerParams(
            collective_id=0, has_side_effects=True, vmem_limit_bytes=48 << 20
        ),
        cost_estimate=pl.CostEstimate(
            flops=1_500_000_000, bytes_accessed=8_000_000, transcendentals=20_000
        ),
        name="sage_layer",
    )(
        features, w_self, w_neigh, bias_vector.reshape(1, -1), cotangent, adj_values,
        src_slots, dst_slots, slot_counts,
    )
    return outs[0], outs[1], outs[2], outs[3], outs[4].reshape(-1)


def solution(mesh):
    placed = (
        P("row", None),
        P(),
        P(),
        P(),
        P("row", None),
        P("row", "rep", None, None, None),
        P("row", "rep", None),
        P("row", "rep", None),
        P("row", "rep"),
    )
    return jax.shard_map(
        shards,
        mesh=mesh,
        in_specs=placed,
        out_specs=(P(("row", "rep"), None), P(("row", "rep"), None), P(), P(), P()),
        check_vma=False,
    )
```

```python
import math

import jax
import jax.numpy as jnp
from jax import lax
from jax.experimental import pallas as pl
from jax.experimental.pallas import tpu as pltpu
from jax.sharding import PartitionSpec as P

RING = 8
HALF = 128
CHUNK = 32
TILE = 128
NB = 512
F = 256
MESH = pl.DeviceIdType.MESH
BF = jnp.bfloat16
F32 = jnp.float32


def wrap(value):
    return lax.rem(value, RING)


def dot_first(a, b):
    return lax.dot_general(a, b, (((0,), (0,)), ((), ())), preferred_element_type=F32)


def dot_last(a, b):
    return lax.dot_general(a, b, (((1,), (1,)), ((), ())), preferred_element_type=F32)


def kernel(
    norm_factor, grad_factor,
    feat_hbm, ws_hbm, wn_hbm, bias_hbm, cot_hbm, adj, src_hbm, dst_hbm, counts,
    act_out, gf_out, gs_out, gn_out, gb_out,
    feat, w_self, w_neigh, cot, bias, src_slots, dst_slots,
    tiles, dense, part, rec_a, rec_b, mid_a, mid_b, rec_a2, rec_b2, agg,
    f_rows, c_rows, g_own, a_own, act_ret, g_ret, gbuf, acc, back, rec_z, b_sib, b_own,
    gp, gp_rec, gx, gx_rec, gy, gz, gfull, gbias,
    load_sem, s_t, r_t, s_adj, r_adj, s_a1, r_a1, s_b1, r_b1, s_a2, r_a2, s_b2, r_b2,
    s_agg, r_agg, s_ga1, r_ga1, s_gb1, r_gb1, s_ga2, r_ga2, s_gb2, r_gb2, s_ret, r_ret,
    s_gz, r_gz, s_gx, r_gx, s_gy, r_gy, s_hx, r_hx, s_hz, r_hz, s_hs, r_hs,
    s_z, r_z, s_sib, r_sib,
):
    row = lax.axis_index("row")
    rep = lax.axis_index("rep")
    y, x = row // RING, lax.rem(row, RING)
    z, k = rep // 2, lax.rem(rep, 2)
    sib = 1 - k

    def at(xx, yy, zz, kk):
        return (yy * RING + xx, zz * 2 + kk)

    def along(axis, d):
        if axis == "x":
            return at(wrap(x + d), y, z, k)
        if axis == "y":
            return at(x, wrap(y + d), z, k)
        return at(x, y, wrap(z + d), k)

    def remote(src, dst, send_sem, recv_sem, device):
        return pltpu.make_async_remote_copy(
            src_ref=src, dst_ref=dst, send_sem=send_sem, recv_sem=recv_sem,
            device_id=device, device_id_type=MESH,
        )

    def peers(fn):
        def step(i, carry):
            fn(4 + (1 - 2 * lax.rem(i, 2)) * ((i + 1) // 2))
            return carry

        lax.fori_loop(0, RING - 1, step, 0)

    def unless(condition, fn):
        pl.when(jnp.logical_not(condition))(fn)

    sent = []

    class Exchange:
        def __init__(self, copy, start=None, recv=None, done=None):
            self.copy = copy
            self.start_all = start or (lambda: peers(lambda d: copy(d).start()))
            self.recv_all = recv or (lambda: peers(lambda d: copy(d).wait_recv()))
            self.done = done or (lambda: peers(lambda d: copy(d).wait_send()))
            self.pending = False

        def start(self):
            self.start_all()
            self.begun()

        def begun(self):
            self.pending = True
            sent.append(self)

        def recv(self):
            self.recv_all()
            self.pending = False

    def single(copy):
        return Exchange(None, copy.start, copy.wait_recv, copy.wait_send)

    def finish():
        for exchange in sent:
            if exchange.pending:
                exchange.recv()
        for exchange in sent:
            exchange.done()

    own_chunk = rep
    worker_y = wrap(own_chunk)
    own_half = own_chunk // RING
    is_self = jnp.logical_and(worker_y == y, y == z)

    def worker(core):
        return at(x, worker_y, y, core)

    def owner(half):
        return at(x, z, 4 * half + y // 2, lax.rem(y, 2))

    def owner_is_self(half):
        return jnp.logical_and(is_self, own_half == half)

    def worker_is_self(core):
        return jnp.logical_and(is_self, k == core)

    load_tiles = [
        pltpu.make_async_copy(
            adj.at[0, 0, pl.ds(16 * part_no, 16)], tiles.at[pl.ds(16 * part_no, 16)],
            load_sem.at[5 + part_no],
        )
        for part_no in range(4)
    ]
    load_feat = pltpu.make_async_copy(feat_hbm, feat, load_sem.at[1])
    load_cot = pltpu.make_async_copy(cot_hbm, cot, load_sem.at[2])
    load_ws = pltpu.make_async_copy(ws_hbm, w_self, load_sem.at[3])
    load_wn = pltpu.make_async_copy(wn_hbm, w_neigh, load_sem.at[4])
    load_bias = pltpu.make_async_copy(bias_hbm, bias, load_sem.at[9])
    load_src = pltpu.make_async_copy(src_hbm, src_slots, load_sem.at[10])
    load_dst = pltpu.make_async_copy(dst_hbm, dst_slots, load_sem.at[11])
    for load in (
        load_src, load_dst, load_feat, *load_tiles, load_cot, load_ws, load_wn, load_bias
    ):
        load.start()

    barrier = pltpu.get_barrier_semaphore()

    def greet(device):
        pl.semaphore_signal(barrier, inc=1, device_id=device, device_id_type=MESH)

    def greet_peers(d):
        for core in (0, 1):
            greet(at(wrap(x + d), y, z, core))
            greet(at(x, wrap(y + d), z, core))
        greet(at(x, y, wrap(z + d), k))

    peers(greet_peers)
    greet(at(x, y, z, sib))
    for core in (0, 1):
        unless(worker_is_self(core), lambda core=core: greet(worker(core)))
        unless(owner_is_self(core), lambda core=core: greet(owner(core)))

    for load in (load_src, load_dst, load_feat, *load_tiles):
        load.wait()

    live = counts[0, 0]

    def build(section, pointer):
        for t in range(4):
            for u in range(4):
                slot = jnp.minimum(pointer, 63)
                hit = jnp.logical_and(
                    pointer < live,
                    jnp.logical_and(
                        src_slots[0, 0, slot] == section * 4 + u, dst_slots[0, 0, slot] == t
                    ),
                )
                tile = tiles[slot]
                dense[4 * k + section, pl.ds(t * TILE, TILE), pl.ds(u * TILE, TILE)] = jnp.where(
                    hit, tile, jnp.zeros_like(tile)
                )
                pointer = pointer + hit.astype(jnp.int32)
        return pointer

    pointer = jnp.int32(0)
    for section in range(4):
        pointer = build(section, pointer)
        product = dot_first(dense[4 * k + section], feat[...]).astype(BF)
        part[0, section] = product[:, :HALF]
        part[1, section] = product[:, HALF:]
    for load in (load_cot, load_ws, load_wn, load_bias):
        load.wait()

    pl.semaphore_wait(barrier, 40 - 2 * is_self.astype(jnp.int32))

    mine_here = (x // 4) == k

    def a1_copy(section, lane):
        to_x = 4 * k + section
        d = wrap(to_x - x + RING)
        return remote(
            part.at[lane, section, pl.ds(0, 256)], rec_a.at[d],
            s_a1.at[section * 2 + lane], r_a1.at[d], at(to_x, y, z, lane),
        )

    def a1_each(method):
        def step(section, carry):
            for lane in (0, 1):
                unless(
                    jnp.logical_and(4 * k + section == x, k == lane),
                    lambda lane=lane: getattr(a1_copy(section, lane), method)(),
                )
            return carry

        lax.fori_loop(0, 4, step, 0)

    def a1_wait(d):
        remote(rec_a.at[d], rec_a.at[d], s_a1.at[0], r_a1.at[d], at(x, y, z, sib)).wait_recv()

    def a1_recv():
        unless(mine_here, lambda: a1_wait(0))
        peers(a1_wait)

    a1 = Exchange(
        None, lambda: a1_each("start"), a1_recv, lambda: a1_each("wait_send")
    )

    def b1_copy(d, lane):
        to_y = wrap(y + d)
        return remote(
            part.at[lane, :, pl.ds(256 + CHUNK * to_y, CHUNK)], rec_b.at[d, k],
            s_b1.at[d * 2 + lane], r_b1.at[d * 2 + k], at(x, to_y, z, lane),
        )

    def b1_start(d):
        for lane in (0, 1):
            b1_copy(d, lane).start()

    def b1_wait(d):
        for core in (0, 1):
            remote(
                rec_b.at[d, core], rec_b.at[d, core], s_b1.at[0], r_b1.at[d * 2 + core],
                at(x, y, z, sib),
            ).wait_recv()

    def b1_done(d):
        for lane in (0, 1):
            b1_copy(d, lane).wait_send()

    b1 = Exchange(
        None, lambda: peers(b1_start), lambda: peers(b1_wait), lambda: peers(b1_done)
    )
    b1_sib = Exchange(
        None,
        lambda: remote(
            part.at[sib, :, pl.ds(256 + CHUNK * y, CHUNK)], rec_b.at[0, k],
            s_b1.at[0], r_b1.at[k], at(x, y, z, sib),
        ).start(),
        lambda: remote(
            rec_b.at[0, sib], rec_b.at[0, sib], s_b1.at[0], r_b1.at[sib], at(x, y, z, sib)
        ).wait_recv(),
        lambda: remote(
            part.at[sib, :, pl.ds(256 + CHUNK * y, CHUNK)], rec_b.at[0, k],
            s_b1.at[0], r_b1.at[k], at(x, y, z, sib),
        ).wait_send(),
    )
    a1.start()
    b1.start()
    b1_sib.start()
    rec_b[0, k] = part[k, :, pl.ds(pl.multiple_of(256 + CHUNK * y, CHUNK), CHUNK), :]

    @pl.when(mine_here)
    def _():
        rec_a[0] = part[k, x - 4 * k, pl.ds(0, 256), :]

    def t_copies(core):
        rows = pl.ds(CHUNK * own_chunk, CHUNK)
        return (
            remote(feat.at[rows], f_rows.at[own_half], s_t.at[core], r_t.at[own_half], worker(core)),
            remote(
                cot.at[rows, pl.ds(HALF * core, HALF)], c_rows.at[own_half],
                s_t.at[2 + core], r_t.at[2 + own_half], worker(core),
            ),
        )

    def t_each(method):
        def step(core):
            for copy in t_copies(core):
                getattr(copy, method)()

        for core in (0, 1):
            unless(worker_is_self(core), lambda core=core: step(core))

    def t_recv():
        def step(half):
            remote(f_rows.at[half], f_rows.at[half], s_t.at[0], r_t.at[half], owner(half)).wait_recv()
            remote(
                c_rows.at[half], c_rows.at[half], s_t.at[2], r_t.at[2 + half], owner(half)
            ).wait_recv()

        for half in (0, 1):
            unless(owner_is_self(half), lambda half=half: step(half))

    fetch = Exchange(None, lambda: t_each("start"), t_recv, lambda: t_each("wait_send"))
    fetch.start()

    @pl.when(is_self)
    def _():
        rows = pl.ds(pl.multiple_of(CHUNK * own_chunk, CHUNK), CHUNK)
        f_rows[own_half] = feat[rows, :]
        c_rows[own_half] = cot[rows, pl.ds(pl.multiple_of(HALF * k, HALF), HALF)]

    adj_swap = single(
        remote(
            dense.at[pl.ds(4 * k, 4)], dense.at[pl.ds(4 * k, 4)], s_adj.at[0], r_adj.at[0],
            at(x, y, z, sib),
        )
    )
    adj_swap.start()

    fetch.recv()
    lanes = pl.ds(pl.multiple_of(HALF * k, HALF), HALF)
    rows64 = f_rows[...].reshape(64, F)
    self_part = jnp.dot(rows64, w_self[:, lanes], preferred_element_type=F32) + bias[:, lanes]

    def summed(ref):
        total = ref[0].astype(F32)
        for d in range(1, RING):
            total = total + ref[d].astype(F32)
        return total

    a1.recv()
    mid_a[...] = summed(rec_a).astype(BF).reshape(RING, CHUNK, HALF)
    a2 = Exchange(
        lambda d: remote(
            mid_a.at[wrap(y + d)], rec_a2.at[d], s_a2.at[d], r_a2.at[d], along("y", d)
        )
    )
    a2.start()
    rec_a2[0] = mid_a[y]

    b1_sib.recv()
    b1.recv()
    mid_b[...] = summed(rec_b).astype(BF).reshape(RING, CHUNK, HALF)
    b2 = Exchange(
        lambda d: remote(
            mid_b.at[wrap(x + d)], rec_b2.at[d], s_b2.at[d], r_b2.at[d], along("x", d)
        )
    )
    b2.start()
    rec_b2[0] = mid_b[x]

    a2.recv()
    agg[k, pl.ds(0, CHUNK), :] = (summed(rec_a2) * norm_factor).astype(BF)
    b2.recv()
    agg[k, pl.ds(CHUNK, CHUNK), :] = (summed(rec_b2) * norm_factor).astype(BF)
    agg_swap = single(remote(agg.at[k], agg.at[k], s_agg.at[0], r_agg.at[0], at(x, y, z, sib)))
    agg_swap.start()
    agg_swap.recv()

    pre = (
        self_part
        + jnp.dot(agg[0], w_neigh[pl.ds(0, HALF), lanes], preferred_element_type=F32)
        + jnp.dot(agg[1], w_neigh[pl.ds(HALF, HALF), lanes], preferred_element_type=F32)
    )
    low = jnp.exp(jnp.minimum(pre, 0.0))
    grad = (c_rows[...].reshape(64, HALF).astype(F32) * low).astype(BF)
    g_own[...] = grad.reshape(2, CHUNK, HALF)

    place_a = gbuf.at[x, pl.ds(CHUNK * y, CHUNK)]
    place_b = gbuf.at[x, pl.ds(256 + CHUNK * y, CHUNK)]
    ga1 = Exchange(
        lambda d: remote(g_own.at[0], place_a, s_ga1.at[d], r_ga1.at[d], along("y", d))
    )
    gb1 = Exchange(
        lambda d: remote(g_own.at[1], place_b, s_gb1.at[d], r_gb1.at[d], along("x", d))
    )
    ga1.start()
    gb1.start()
    gbuf[x, pl.ds(pl.multiple_of(CHUNK * y, CHUNK), CHUNK), :] = g_own[0]
    gbuf[x, pl.ds(pl.multiple_of(256 + CHUNK * y, CHUNK), CHUNK), :] = g_own[1]
    a_own[...] = jnp.where(pre > 0, pre, low - 1.0).astype(BF).reshape(2, CHUNK, HALF)

    def ret_copies(half):
        return (
            remote(a_own.at[half], act_ret.at[k], s_ret.at[half], r_ret.at[k], owner(half)),
            remote(g_own.at[half], g_ret.at[k], s_ret.at[2 + half], r_ret.at[2 + k], owner(half)),
        )

    def ret_each(method):
        def step(half):
            for copy in ret_copies(half):
                getattr(copy, method)()

        for half in (0, 1):
            unless(owner_is_self(half), lambda half=half: step(half))

    def ret_recv():
        def step(core):
            remote(
                act_ret.at[core], act_ret.at[core], s_ret.at[0], r_ret.at[core], worker(core)
            ).wait_recv()
            remote(
                g_ret.at[core], g_ret.at[core], s_ret.at[2], r_ret.at[2 + core], worker(core)
            ).wait_recv()

        for core in (0, 1):
            unless(worker_is_self(core), lambda core=core: step(core))

    give_back = Exchange(None, lambda: ret_each("start"), ret_recv, lambda: ret_each("wait_send"))
    give_back.start()

    @pl.when(is_self)
    def _():
        act_ret[k] = a_own[own_half]
        g_ret[k] = g_own[own_half]

    grad_s = dot_first(rows64, grad)
    grad_n = jnp.concatenate([dot_first(agg[0], grad), dot_first(agg[1], grad)], 0)
    terms = jnp.concatenate([grad_s, grad_n], 0).reshape(RING, 64, HALF)
    gp[:, pl.ds(0, 64), :] = terms
    col_sum = jnp.broadcast_to(jnp.sum(grad.astype(F32), axis=0, keepdims=True), (8, HALF))
    gp[:, pl.ds(64, 8), :] = jnp.broadcast_to(col_sum[None], (RING, 8, HALF))
    to_z = Exchange(
        lambda d: remote(gp.at[wrap(z + d)], gp_rec.at[z], s_gz.at[d], r_gz.at[d], along("z", d))
    )
    to_z.start()
    gp_rec[z] = gp[z]

    class Relay:
        def __init__(self, axis, me, piece, half, send_sem, recv_sem):
            self.axis, self.me, self.piece, self.half = axis, me, piece, half
            self.sems = (send_sem, recv_sem)
            self.pending = False
            self.done_all = []

        def copy(self, ref, sign, hop, tag):
            send_sem, recv_sem = self.sems
            index = 2 * tag + (sign < 0)
            return remote(
                ref, ref, send_sem.at[index], recv_sem.at[index],
                along(self.axis, (sign * hop) % RING),
            )

        def owner(self, sign, distance):
            return wrap(self.me + (-sign * distance) % RING)

        def near(self, sign):
            return self.copy(self.piece(self.me), sign, 1, 0)

        def next_near(self, sign):
            return self.copy(self.piece(self.me), sign, 2, 1)

        def far(self, sign):
            return self.copy(self.piece(self.owner(sign, 2)), sign, 1, 2)

        def opposite(self, sign):
            return self.copy(self.half(self.owner(sign, 2), sign), sign, 2, 3)

        def start(self):
            for sign in (1, -1):
                self.next_near(sign).start()
            for sign in (1, -1):
                self.near(sign).start()
            self.pending = True
            sent.append(self)

        def pass_on(self):
            for sign in (1, -1):
                self.next_near(sign).wait_recv()
                self.opposite(sign).start()
                self.far(sign).start()

        def recv(self):
            for sign in (1, -1):
                self.near(sign).wait_recv()
                self.far(sign).wait_recv()
                self.opposite(sign).wait_recv()
            self.pending = False

        def done(self):
            for sign in (1, -1):
                for copy in (self.near, self.next_near, self.far, self.opposite):
                    copy(sign).wait_send()

    ga2 = Relay(
        "x", x, lambda at_x: gbuf.at[at_x, pl.ds(0, 256)],
        lambda at_x, sign: gbuf.at[at_x, pl.ds(0 if sign > 0 else 128, 128)], s_ga2, r_ga2,
    )
    gb2 = Relay(
        "y", y, lambda at_y: gbuf.at[:, pl.ds(256 + CHUNK * at_y, CHUNK)],
        lambda at_y, sign: gbuf.at[
            pl.ds(0 if sign > 0 else 4, 4), pl.ds(256 + CHUNK * at_y, CHUNK)
        ], s_gb2, r_gb2,
    )
    ga1.recv()
    ga2.start()
    gb1.recv()
    gb2.start()
    ga2.pass_on()
    gb2.pass_on()

    to_z.recv()
    over_z = summed(gp_rec)
    gx[:, pl.ds(0, 8), :] = over_z[:64].reshape(RING, 8, HALF)
    gx[:, pl.ds(8, 8), :] = jnp.broadcast_to(over_z[64:][None], (RING, 8, HALF))
    to_x = Exchange(
        lambda d: remote(gx.at[wrap(x + d)], gx_rec.at[x], s_gx.at[d], r_gx.at[d], along("x", d))
    )
    to_x.start()
    gx_rec[x] = gx[x]

    adj_swap.recv()

    def pull(at_x, first):
        acc[...] += jnp.dot(
            dense[at_x, :, pl.ds(first, 256)], gbuf[at_x, pl.ds(first, 256), :],
            preferred_element_type=F32,
        )

    acc[...] = jnp.zeros_like(acc)
    pull(x, 0)

    for sign in (1, -1):
        pull(ga2.owner(sign, 2), 0)
    for sign in (1, -1):
        ga2.near(sign).wait_recv()
        pull(ga2.owner(sign, 1), 0)
    for sign in (1, -1):
        ga2.far(sign).wait_recv()
        pull(ga2.owner(sign, 3), 0)
    for sign in (1, -1):
        ga2.opposite(sign).wait_recv()
    ga2.pending = False
    pull(ga2.owner(1, 4), 0)

    to_x.recv()
    gy[y] = summed(gx_rec)
    over_y = Exchange(lambda d: remote(gy.at[y], gy.at[y], s_gy.at[d], r_gy.at[d], along("y", d)))
    over_y.start()

    gb2.recv()
    lax.fori_loop(0, RING, lambda at_x, carry: (pull(at_x, 256), carry)[1], 0)
    back[...] = acc[...].astype(BF).reshape(RING, 64, HALF)
    sums = Exchange(
        lambda d: remote(back.at[wrap(z + d)], rec_z.at[d], s_z.at[d], r_z.at[d], along("z", d))
    )
    sums.start()
    rec_z[0] = back[z]

    over_y.recv()
    total_y = summed(gy)
    gz[x] = total_y[:8]
    gbias[k] = total_y[8:]
    from_x = Exchange(lambda d: remote(gz.at[x], gz.at[x], s_hx.at[d], r_hx.at[d], along("x", d)))
    from_x.start()
    bias_swap = single(remote(gbias.at[k], gbias.at[k], s_hs.at[1], r_hs.at[1], at(x, y, z, sib)))
    bias_swap.start()

    sums.recv()
    b_own[...] = summed(rec_z).astype(BF).reshape(2, CHUNK, HALF)
    b_swap = single(remote(b_own.at[sib], b_sib, s_sib.at[0], r_sib.at[0], at(x, y, z, sib)))
    b_swap.start()

    from_x.recv()
    gfull[k, z] = gz[...].reshape(64, HALF).astype(BF)
    from_z = Exchange(
        lambda d: remote(gfull.at[k, z], gfull.at[k, z], s_hz.at[d], r_hz.at[d], along("z", d))
    )
    from_z.start()

    give_back.recv()
    act_out[:, pl.ds(0, HALF)] = act_ret[0]
    act_out[:, pl.ds(HALF, HALF)] = act_ret[1]
    own_part = dot_last(g_ret[0], w_self[:, pl.ds(0, HALF)]) + dot_last(
        g_ret[1], w_self[:, pl.ds(HALF, HALF)]
    )
    b_swap.recv()
    returned = dot_last(b_own[k], w_neigh[:, lanes]) + dot_last(
        b_sib[...], w_neigh[:, pl.ds(pl.multiple_of(HALF * sib, HALF), HALF)]
    )
    gf_out[...] = (own_part + returned * norm_factor).astype(BF)

    from_z.recv()
    full_swap = single(remote(gfull.at[k], gfull.at[k], s_hs.at[0], r_hs.at[0], at(x, y, z, sib)))
    full_swap.start()
    bias_swap.recv()
    for core in (0, 1):
        gb_out[:, pl.ds(HALF * core, HALF)] = gbias[core, pl.ds(0, 1), :] * grad_factor
    full_swap.recv()
    for core in (0, 1):
        gs_out[:, pl.ds(HALF * core, HALF)] = (
            gfull[core, pl.ds(0, 4)].reshape(F, HALF).astype(F32) * grad_factor
        )
        gn_out[:, pl.ds(HALF * core, HALF)] = (
            gfull[core, pl.ds(4, 4)].reshape(F, HALF).astype(F32) * grad_factor
        )
    finish()


def place(*refs):
    copies = [
        pltpu.make_async_copy(refs[i], refs[5 + i], refs[10].at[i]) for i in range(5)
    ]
    for copy in copies:
        copy.start()
    for copy in copies:
        copy.wait()


def shards(
    features, w_self, w_neigh, bias_vector, cotangent, adj_values, src_slots, dst_slots, slot_counts
):
    block_rows = features.shape[0]
    replicas = lax.axis_size("rep")
    node_total = block_rows * lax.axis_size("row")
    slot_total = adj_values.shape[2]
    norm_factor = 1.0 / math.sqrt(slot_total * replicas / (block_rows // adj_values.shape[-1]))
    grad_factor = 1.0 / math.sqrt(node_total)

    def body(*refs):
        kernel(norm_factor, grad_factor, *refs)

    vmem = pl.BlockSpec(memory_space=pltpu.VMEM)
    hbm = pl.BlockSpec(memory_space=pltpu.HBM)
    smem = pl.BlockSpec(memory_space=pltpu.SMEM)
    dma = pltpu.SemaphoreType.DMA
    sems = [
        dma((12,)), dma((4,)), dma((4,)), dma((1,)), dma((1,)), dma((8,)), dma((8,)), dma((16,)),
        dma((16,)), dma((8,)), dma((8,)), dma((8,)), dma((8,)),
        dma((1,)), dma((1,)), dma((8,)), dma((8,)), dma((8,)), dma((8,)), dma((8,)), dma((8,)),
        dma((8,)), dma((8,)), dma((4,)), dma((4,)),
        dma((8,)), dma((8,)), dma((8,)), dma((8,)), dma((8,)), dma((8,)), dma((8,)), dma((8,)),
        dma((8,)), dma((8,)), dma((2,)), dma((2,)),
        dma((8,)), dma((8,)), dma((1,)), dma((1,)),
    ]
    scratch = [
        pltpu.VMEM((NB, F), BF),
        pltpu.VMEM((F, F), BF),
        pltpu.VMEM((F, F), BF),
        pltpu.VMEM((NB, F), BF),
        pltpu.VMEM((1, F), F32),
        pltpu.SMEM((1, 1, 64), jnp.int32),
        pltpu.SMEM((1, 1, 64), jnp.int32),
        pltpu.VMEM((64, TILE, TILE), BF),
        pltpu.VMEM((8, NB, NB), BF),
        pltpu.VMEM((2, 4, NB, HALF), BF),
        pltpu.VMEM((8, 256, HALF), BF),
        pltpu.VMEM((8, 2, 4, CHUNK, HALF), BF),
        pltpu.VMEM((8, CHUNK, HALF), BF),
        pltpu.VMEM((8, CHUNK, HALF), BF),
        pltpu.VMEM((8, CHUNK, HALF), BF),
        pltpu.VMEM((8, CHUNK, HALF), BF),
        pltpu.VMEM((2, 64, HALF), BF),
        pltpu.VMEM((2, CHUNK, F), BF),
        pltpu.VMEM((2, CHUNK, HALF), BF),
        pltpu.VMEM((2, CHUNK, HALF), BF),
        pltpu.VMEM((2, CHUNK, HALF), BF),
        pltpu.VMEM((2, CHUNK, HALF), BF),
        pltpu.VMEM((2, CHUNK, HALF), BF),
        pltpu.VMEM((8, NB, HALF), BF),
        pltpu.VMEM((NB, HALF), F32),
        pltpu.VMEM((8, 64, HALF), BF),
        pltpu.VMEM((8, 64, HALF), BF),
        pltpu.VMEM((CHUNK, HALF), BF),
        pltpu.VMEM((2, CHUNK, HALF), BF),
        pltpu.VMEM((8, 72, HALF), F32),
        pltpu.VMEM((8, 72, HALF), F32),
        pltpu.VMEM((8, 16, HALF), F32),
        pltpu.VMEM((8, 16, HALF), F32),
        pltpu.VMEM((8, 16, HALF), F32),
        pltpu.VMEM((8, 8, HALF), F32),
        pltpu.VMEM((2, 8, 64, HALF), BF),
        pltpu.VMEM((2, 8, HALF), F32),
    ]
    outs = pl.pallas_call(
        body,
        out_shape=(
            jax.ShapeDtypeStruct((CHUNK, F), BF),
            jax.ShapeDtypeStruct((CHUNK, F), BF),
            jax.ShapeDtypeStruct((F, F), F32),
            jax.ShapeDtypeStruct((F, F), F32),
            jax.ShapeDtypeStruct((1, F), F32),
        ),
        in_specs=[hbm] * 8 + [smem],
        out_specs=(vmem,) * 5,
        scratch_shapes=scratch + sems,
        compiler_params=pltpu.CompilerParams(
            collective_id=0, has_side_effects=True, vmem_limit_bytes=48 << 20
        ),
        cost_estimate=pl.CostEstimate(
            flops=1_500_000_000, bytes_accessed=8_000_000, transcendentals=20_000
        ),
        name="sage_layer",
    )(
        *(
            pltpu.with_memory_space_constraint(array, pltpu.HBM)
            for array in (
                features, w_self, w_neigh, bias_vector.reshape(1, -1), cotangent, adj_values,
                src_slots, dst_slots,
            )
        ),
        slot_counts,
    )
    act, gf, gs, gn, gb = pl.pallas_call(
        place,
        out_shape=tuple(jax.ShapeDtypeStruct(out.shape, out.dtype) for out in outs),
        in_specs=[vmem] * 5,
        out_specs=(hbm,) * 5,
        scratch_shapes=[dma((5,))],
        compiler_params=pltpu.CompilerParams(vmem_limit_bytes=4 << 20),
        name="place_results",
    )(*outs)
    return act, gf, gs, gn, gb.reshape(-1)


def solution(mesh):
    placed = (
        P("row", None),
        P(),
        P(),
        P(),
        P("row", None),
        P("row", "rep", None, None, None),
        P("row", "rep", None),
        P("row", "rep", None),
        P("row", "rep"),
    )
    return jax.shard_map(
        shards,
        mesh=mesh,
        in_specs=placed,
        out_specs=(P(("row", "rep"), None), P(("row", "rep"), None), P(), P(), P()),
        check_vma=False,
    )
```

```python
import math

import jax
import jax.numpy as jnp
from jax import lax
from jax.experimental import pallas as pl
from jax.experimental.pallas import tpu as pltpu
from jax.sharding import PartitionSpec as P

RING = 8
HALF = 128
CHUNK = 32
TILE = 128
NB = 512
F = 256
MESH = pl.DeviceIdType.MESH
BF = jnp.bfloat16
F32 = jnp.float32


def wrap(value):
    return lax.rem(value, RING)


def dot_first(a, b):
    return lax.dot_general(a, b, (((0,), (0,)), ((), ())), preferred_element_type=F32)


def dot_last(a, b):
    return lax.dot_general(a, b, (((1,), (1,)), ((), ())), preferred_element_type=F32)


def kernel(
    norm_factor, grad_factor,
    feat_hbm, ws_hbm, wn_hbm, bias_hbm, cot_hbm, adj, src_hbm, dst_hbm, counts,
    act_out, gf_out, gs_out, gn_out, gb_out,
    feat, w_self, w_neigh, cot, bias, src_slots, dst_slots,
    tiles, dense, part, rec_a, rec_b, mid_a, mid_b, rec_a2, rec_b2, agg,
    rel_a3, rel_a4, comb_a, rel_b3, rel_b4, comb_b,
    f_rows, c_rows, g_own, a_own, act_ret, g_ret, gbuf, acc, back, rec_z, b_sib, b_own,
    gp, gp_rec, gx, gx_rec, gy, gz, gfull, gbias,
    load_sem, s_t, r_t, s_adj, r_adj, s_a1, r_a1, s_b1, r_b1, s_a2, r_a2, s_b2, r_b2,
    s_agg, r_agg, s_ga1, r_ga1, s_gb1, r_gb1, s_ga2, r_ga2, s_gb2, r_gb2, s_ret, r_ret,
    s_gz, r_gz, s_gx, r_gx, s_gy, r_gy, s_hx, r_hx, s_hz, r_hz, s_hs, r_hs,
    s_z, r_z, s_sib, r_sib,
):
    row = lax.axis_index("row")
    rep = lax.axis_index("rep")
    y, x = row // RING, lax.rem(row, RING)
    z, k = rep // 2, lax.rem(rep, 2)
    sib = 1 - k

    def at(xx, yy, zz, kk):
        return (yy * RING + xx, zz * 2 + kk)

    def along(axis, d):
        if axis == "x":
            return at(wrap(x + d), y, z, k)
        if axis == "y":
            return at(x, wrap(y + d), z, k)
        return at(x, y, wrap(z + d), k)

    def remote(src, dst, send_sem, recv_sem, device):
        return pltpu.make_async_remote_copy(
            src_ref=src, dst_ref=dst, send_sem=send_sem, recv_sem=recv_sem,
            device_id=device, device_id_type=MESH,
        )

    def peers(fn):
        def step(i, carry):
            fn(4 + (1 - 2 * lax.rem(i, 2)) * ((i + 1) // 2))
            return carry

        lax.fori_loop(0, RING - 1, step, 0)

    def unless(condition, fn):
        pl.when(jnp.logical_not(condition))(fn)

    sent = []

    class Exchange:
        def __init__(self, copy, start=None, recv=None, done=None):
            self.copy = copy
            self.start_all = start or (lambda: peers(lambda d: copy(d).start()))
            self.recv_all = recv or (lambda: peers(lambda d: copy(d).wait_recv()))
            self.done = done or (lambda: peers(lambda d: copy(d).wait_send()))
            self.pending = False

        def start(self):
            self.start_all()
            self.begun()

        def begun(self):
            self.pending = True
            sent.append(self)

        def recv(self):
            self.recv_all()
            self.pending = False

    def single(copy):
        return Exchange(None, copy.start, copy.wait_recv, copy.wait_send)

    def finish():
        for exchange in sent:
            if exchange.pending:
                exchange.recv()
        for exchange in sent:
            exchange.done()

    own_chunk = rep
    worker_y = wrap(own_chunk)
    own_half = own_chunk // RING
    is_self = jnp.logical_and(worker_y == y, y == z)

    def worker(core):
        return at(x, worker_y, y, core)

    def owner(half):
        return at(x, z, 4 * half + y // 2, lax.rem(y, 2))

    def owner_is_self(half):
        return jnp.logical_and(is_self, own_half == half)

    def worker_is_self(core):
        return jnp.logical_and(is_self, k == core)

    load_tiles = [
        pltpu.make_async_copy(
            adj.at[0, 0, pl.ds(16 * part_no, 16)], tiles.at[pl.ds(16 * part_no, 16)],
            load_sem.at[5 + part_no],
        )
        for part_no in range(4)
    ]
    load_feat = pltpu.make_async_copy(feat_hbm, feat, load_sem.at[1])
    load_cot = pltpu.make_async_copy(cot_hbm, cot, load_sem.at[2])
    load_ws = pltpu.make_async_copy(ws_hbm, w_self, load_sem.at[3])
    load_wn = pltpu.make_async_copy(wn_hbm, w_neigh, load_sem.at[4])
    load_bias = pltpu.make_async_copy(bias_hbm, bias, load_sem.at[9])
    load_src = pltpu.make_async_copy(src_hbm, src_slots, load_sem.at[10])
    load_dst = pltpu.make_async_copy(dst_hbm, dst_slots, load_sem.at[11])
    for load in (
        load_src, load_dst, load_feat, *load_tiles, load_cot, load_ws, load_wn, load_bias
    ):
        load.start()

    barrier = pltpu.get_barrier_semaphore()

    def greet(device):
        pl.semaphore_signal(barrier, inc=1, device_id=device, device_id_type=MESH)

    def greet_peers(d):
        for axis in ("x", "y", "z"):
            greet(along(axis, d))

    peers(greet_peers)
    for d in (1, 2, RING - 2, RING - 1):
        greet(at(wrap(x + d), y, z, sib))
        greet(at(x, wrap(y + d), z, sib))
    greet(at(x, y, z, sib))
    for core in (0, 1):
        unless(worker_is_self(core), lambda core=core: greet(worker(core)))
        unless(owner_is_self(core), lambda core=core: greet(owner(core)))

    for load in (load_src, load_dst, load_feat, *load_tiles):
        load.wait()

    live = counts[0, 0]

    def build(section, pointer):
        for t in range(4):
            for u in range(4):
                slot = jnp.minimum(pointer, 63)
                hit = jnp.logical_and(
                    pointer < live,
                    jnp.logical_and(
                        src_slots[0, 0, slot] == section * 4 + u, dst_slots[0, 0, slot] == t
                    ),
                )
                tile = tiles[slot]
                dense[4 * k + section, pl.ds(t * TILE, TILE), pl.ds(u * TILE, TILE)] = jnp.where(
                    hit, tile, jnp.zeros_like(tile)
                )
                pointer = pointer + hit.astype(jnp.int32)
        return pointer

    pointer = jnp.int32(0)
    for section in range(4):
        pointer = build(section, pointer)
        product = dot_first(dense[4 * k + section], feat[...]).astype(BF)
        part[0, section] = product[:, :HALF]
        part[1, section] = product[:, HALF:]
    for load in (load_cot, load_ws, load_wn, load_bias):
        load.wait()

    pl.semaphore_wait(barrier, 34 - 2 * is_self.astype(jnp.int32))

    mine_here = (x // 4) == k

    class Reduce:
        def __init__(self, axis, term, here, slot, rel3, rel4, comb, send_sem, recv_sem, width):
            self.axis, self.term, self.here, self.slot = axis, term, here, slot
            self.rel3, self.rel4, self.comb = rel3, rel4, comb
            self.send_sem, self.recv_sem, self.width = send_sem, recv_sem, width
            self.pending = False

        def to(self, d, core):
            if self.axis == "x":
                return at(wrap(x + d), y, z, core)
            return at(x, wrap(y + d), z, core)

        def slot_sem(self, number, core):
            return self.recv_sem.at[4 + number * self.width + (core if self.width == 2 else 0)]

        def copies(self, d):
            send, recv = self.send_sem, self.recv_sem
            if d == 4:
                return [
                    remote(
                        self.term(4).at[way], self.rel4.at[way], send.at[way], recv.at[way],
                        self.to(6 if way else 2, k),
                    )
                    for way in (0, 1)
                ]
            if d in (3, 5):
                way = 0 if d == 3 else 1
                return [
                    remote(
                        self.term(d), self.rel3.at[way], send.at[2 + way], recv.at[2 + way],
                        self.to(7 if way else 1, k),
                    )
                ]
            if d == 0:
                return [
                    remote(
                        self.term(0).at[sib], self.slot(0, k), send.at[12], self.slot_sem(0, k),
                        self.to(0, sib),
                    )
                ]
            number = {1: 1, 7: 2, 2: 3, 6: 4}[d]
            source = self.term(d) if number < 3 else self.comb.at[number - 3]
            return [
                remote(
                    source.at[lane], self.slot(number, k), send.at[2 + 2 * number + lane],
                    self.slot_sem(number, k), self.to(d, lane),
                )
                for lane in (0, 1)
            ]

        def when_here(self, d, fn):
            condition = self.here(d)
            if condition is None:
                fn()
            else:
                pl.when(condition)(fn)

        def each(self, method, *distances):
            def step(d):
                for copy in self.copies(d):
                    getattr(copy, method)()

            for d in distances:
                self.when_here(d, lambda d=d: step(d))

        def start(self):
            self.each("start", 4, 3, 5, 1, 7, 0)
            self.pending = True
            sent.append(self)

        def pass_on(self):
            def step(way, d):
                own, rel3, rel4 = self.term(d), self.rel3.at[way], self.rel4.at[way]
                remote(rel4, rel4, self.send_sem.at[0], self.recv_sem.at[way], self.to(0, sib)).wait_recv()
                remote(
                    rel3, rel3, self.send_sem.at[0], self.recv_sem.at[2 + way], self.to(0, sib)
                ).wait_recv()
                for lane in (0, 1):
                    total = own[lane].astype(F32) + rel3[lane].astype(F32)
                    if lane == way:
                        total = total + rel4[...].astype(F32)
                    self.comb[way, lane] = total.astype(BF)
                for copy in self.copies(d):
                    copy.start()

            for way, d in ((0, 2), (1, 6)):
                self.when_here(d, lambda way=way, d=d: step(way, d))

        def wait_slot(self, number, core):
            place = self.slot(number, core)
            remote(
                place, place, self.send_sem.at[0], self.slot_sem(number, core), self.to(0, sib)
            ).wait_recv()

        def recv(self):
            if self.width == 2:
                self.wait_slot(0, sib)
            else:
                unless(mine_here, lambda: self.wait_slot(0, 0))
            for number in (1, 2, 3, 4):
                for core in range(self.width):
                    self.wait_slot(number, core)
            self.pending = False

        def done(self):
            self.each("wait_send", *range(RING))

    def term_a(d):
        return part.at[:, lax.rem(x + d, 4), pl.ds(0, 256)]

    def term_b(d):
        return part.at[:, :, pl.ds(pl.multiple_of(256 + CHUNK * wrap(y + d), CHUNK), CHUNK)]

    a1 = Reduce(
        "x", term_a, lambda d: (wrap(x + d) // 4) == k, lambda number, core: rec_a.at[number],
        rel_a3, rel_a4, comb_a, s_a1, r_a1, 1,
    )
    b1 = Reduce(
        "y", term_b, lambda d: None, lambda number, core: rec_b.at[number, core],
        rel_b3, rel_b4, comb_b, s_b1, r_b1, 2,
    )
    a1.start()
    b1.start()
    rec_b[0, k] = part[k, :, pl.ds(pl.multiple_of(256 + CHUNK * y, CHUNK), CHUNK), :]

    @pl.when(mine_here)
    def _():
        rec_a[0] = part[k, x - 4 * k, pl.ds(0, 256), :]

    def t_copies(core):
        rows = pl.ds(CHUNK * own_chunk, CHUNK)
        return (
            remote(feat.at[rows], f_rows.at[own_half], s_t.at[core], r_t.at[own_half], worker(core)),
            remote(
                cot.at[rows, pl.ds(HALF * core, HALF)], c_rows.at[own_half],
                s_t.at[2 + core], r_t.at[2 + own_half], worker(core),
            ),
        )

    def t_each(method):
        def step(core):
            for copy in t_copies(core):
                getattr(copy, method)()

        for core in (0, 1):
            unless(worker_is_self(core), lambda core=core: step(core))

    def t_recv():
        def step(half):
            remote(f_rows.at[half], f_rows.at[half], s_t.at[0], r_t.at[half], owner(half)).wait_recv()
            remote(
                c_rows.at[half], c_rows.at[half], s_t.at[2], r_t.at[2 + half], owner(half)
            ).wait_recv()

        for half in (0, 1):
            unless(owner_is_self(half), lambda half=half: step(half))

    fetch = Exchange(None, lambda: t_each("start"), t_recv, lambda: t_each("wait_send"))
    fetch.start()

    @pl.when(is_self)
    def _():
        rows = pl.ds(pl.multiple_of(CHUNK * own_chunk, CHUNK), CHUNK)
        f_rows[own_half] = feat[rows, :]
        c_rows[own_half] = cot[rows, pl.ds(pl.multiple_of(HALF * k, HALF), HALF)]

    adj_swap = single(
        remote(
            dense.at[pl.ds(4 * k, 4)], dense.at[pl.ds(4 * k, 4)], s_adj.at[0], r_adj.at[0],
            at(x, y, z, sib),
        )
    )
    adj_swap.start()
    a1.pass_on()
    b1.pass_on()

    fetch.recv()
    lanes = pl.ds(pl.multiple_of(HALF * k, HALF), HALF)
    rows64 = f_rows[...].reshape(64, F)
    self_part = jnp.dot(rows64, w_self[:, lanes], preferred_element_type=F32) + bias[:, lanes]

    def summed(ref):
        total = ref[0].astype(F32)
        for d in range(1, ref.shape[0]):
            total = total + ref[d].astype(F32)
        return total

    a1.recv()
    mid_a[...] = summed(rec_a).astype(BF).reshape(RING, CHUNK, HALF)
    a2 = Exchange(
        lambda d: remote(
            mid_a.at[wrap(y + d)], rec_a2.at[d], s_a2.at[d], r_a2.at[d], along("y", d)
        )
    )
    a2.start()
    rec_a2[0] = mid_a[y]

    b1.recv()
    mid_b[...] = summed(rec_b).astype(BF).reshape(RING, CHUNK, HALF)
    b2 = Exchange(
        lambda d: remote(
            mid_b.at[wrap(x + d)], rec_b2.at[d], s_b2.at[d], r_b2.at[d], along("x", d)
        )
    )
    b2.start()
    rec_b2[0] = mid_b[x]

    a2.recv()
    agg[k, pl.ds(0, CHUNK), :] = (summed(rec_a2) * norm_factor).astype(BF)
    b2.recv()
    agg[k, pl.ds(CHUNK, CHUNK), :] = (summed(rec_b2) * norm_factor).astype(BF)
    agg_swap = single(remote(agg.at[k], agg.at[k], s_agg.at[0], r_agg.at[0], at(x, y, z, sib)))
    agg_swap.start()
    agg_swap.recv()

    pre = (
        self_part
        + jnp.dot(agg[0], w_neigh[pl.ds(0, HALF), lanes], preferred_element_type=F32)
        + jnp.dot(agg[1], w_neigh[pl.ds(HALF, HALF), lanes], preferred_element_type=F32)
    )
    low = jnp.exp(jnp.minimum(pre, 0.0))
    grad = (c_rows[...].reshape(64, HALF).astype(F32) * low).astype(BF)
    g_own[...] = grad.reshape(2, CHUNK, HALF)

    place_a = gbuf.at[x, pl.ds(CHUNK * y, CHUNK)]
    place_b = gbuf.at[x, pl.ds(256 + CHUNK * y, CHUNK)]
    ga1 = Exchange(
        lambda d: remote(g_own.at[0], place_a, s_ga1.at[d], r_ga1.at[d], along("y", d))
    )
    gb1 = Exchange(
        lambda d: remote(g_own.at[1], place_b, s_gb1.at[d], r_gb1.at[d], along("x", d))
    )
    ga1.start()
    gb1.start()
    gbuf[x, pl.ds(pl.multiple_of(CHUNK * y, CHUNK), CHUNK), :] = g_own[0]
    gbuf[x, pl.ds(pl.multiple_of(256 + CHUNK * y, CHUNK), CHUNK), :] = g_own[1]
    a_own[...] = jnp.where(pre > 0, pre, low - 1.0).astype(BF).reshape(2, CHUNK, HALF)

    def ret_copies(half):
        return (
            remote(a_own.at[half], act_ret.at[k], s_ret.at[half], r_ret.at[k], owner(half)),
            remote(g_own.at[half], g_ret.at[k], s_ret.at[2 + half], r_ret.at[2 + k], owner(half)),
        )

    def ret_each(method):
        def step(half):
            for copy in ret_copies(half):
                getattr(copy, method)()

        for half in (0, 1):
            unless(owner_is_self(half), lambda half=half: step(half))

    def ret_recv():
        def step(core):
            remote(
                act_ret.at[core], act_ret.at[core], s_ret.at[0], r_ret.at[core], worker(core)
            ).wait_recv()
            remote(
                g_ret.at[core], g_ret.at[core], s_ret.at[2], r_ret.at[2 + core], worker(core)
            ).wait_recv()

        for core in (0, 1):
            unless(worker_is_self(core), lambda core=core: step(core))

    give_back = Exchange(None, lambda: ret_each("start"), ret_recv, lambda: ret_each("wait_send"))
    give_back.start()

    @pl.when(is_self)
    def _():
        act_ret[k] = a_own[own_half]
        g_ret[k] = g_own[own_half]

    grad_s = dot_first(rows64, grad)
    grad_n = jnp.concatenate([dot_first(agg[0], grad), dot_first(agg[1], grad)], 0)
    terms = jnp.concatenate([grad_s, grad_n], 0).reshape(RING, 64, HALF)
    gp[:, pl.ds(0, 64), :] = terms
    col_sum = jnp.broadcast_to(jnp.sum(grad.astype(F32), axis=0, keepdims=True), (8, HALF))
    gp[:, pl.ds(64, 8), :] = jnp.broadcast_to(col_sum[None], (RING, 8, HALF))
    to_z = Exchange(
        lambda d: remote(gp.at[wrap(z + d)], gp_rec.at[z], s_gz.at[d], r_gz.at[d], along("z", d))
    )
    to_z.start()
    gp_rec[z] = gp[z]

    class Relay:
        def __init__(self, axis, me, piece, half, send_sem, recv_sem):
            self.axis, self.me, self.piece, self.half = axis, me, piece, half
            self.sems = (send_sem, recv_sem)
            self.pending = False
            self.done_all = []

        def copy(self, ref, sign, hop, tag):
            send_sem, recv_sem = self.sems
            index = 2 * tag + (sign < 0)
            return remote(
                ref, ref, send_sem.at[index], recv_sem.at[index],
                along(self.axis, (sign * hop) % RING),
            )

        def owner(self, sign, distance):
            return wrap(self.me + (-sign * distance) % RING)

        def near(self, sign):
            return self.copy(self.piece(self.me), sign, 1, 0)

        def next_near(self, sign):
            return self.copy(self.piece(self.me), sign, 2, 1)

        def far(self, sign):
            return self.copy(self.piece(self.owner(sign, 2)), sign, 1, 2)

        def opposite(self, sign):
            return self.copy(self.half(self.owner(sign, 2), sign), sign, 2, 3)

        def start(self):
            for sign in (1, -1):
                self.next_near(sign).start()
            for sign in (1, -1):
                self.near(sign).start()
            self.pending = True
            sent.append(self)

        def pass_on(self):
            for sign in (1, -1):
                self.next_near(sign).wait_recv()
                self.opposite(sign).start()
                self.far(sign).start()

        def recv(self):
            for sign in (1, -1):
                self.near(sign).wait_recv()
                self.far(sign).wait_recv()
                self.opposite(sign).wait_recv()
            self.pending = False

        def done(self):
            for sign in (1, -1):
                for copy in (self.near, self.next_near, self.far, self.opposite):
                    copy(sign).wait_send()

    ga2 = Relay(
        "x", x, lambda at_x: gbuf.at[at_x, pl.ds(0, 256)],
        lambda at_x, sign: gbuf.at[at_x, pl.ds(0 if sign > 0 else 128, 128)], s_ga2, r_ga2,
    )
    gb2 = Relay(
        "y", y, lambda at_y: gbuf.at[:, pl.ds(256 + CHUNK * at_y, CHUNK)],
        lambda at_y, sign: gbuf.at[
            pl.ds(0 if sign > 0 else 4, 4), pl.ds(256 + CHUNK * at_y, CHUNK)
        ], s_gb2, r_gb2,
    )
    ga1.recv()
    ga2.start()
    gb1.recv()
    gb2.start()
    ga2.pass_on()
    gb2.pass_on()

    to_z.recv()
    over_z = summed(gp_rec)
    gx[:, pl.ds(0, 8), :] = over_z[:64].reshape(RING, 8, HALF)
    gx[:, pl.ds(8, 8), :] = jnp.broadcast_to(over_z[64:][None], (RING, 8, HALF))
    to_x = Exchange(
        lambda d: remote(gx.at[wrap(x + d)], gx_rec.at[x], s_gx.at[d], r_gx.at[d], along("x", d))
    )
    to_x.start()
    gx_rec[x] = gx[x]

    adj_swap.recv()

    def pull(at_x, first):
        acc[...] += jnp.dot(
            dense[at_x, :, pl.ds(first, 256)], gbuf[at_x, pl.ds(first, 256), :],
            preferred_element_type=F32,
        )

    acc[...] = jnp.zeros_like(acc)
    pull(x, 0)

    for sign in (1, -1):
        pull(ga2.owner(sign, 2), 0)
    for sign in (1, -1):
        ga2.near(sign).wait_recv()
        pull(ga2.owner(sign, 1), 0)
    for sign in (1, -1):
        ga2.far(sign).wait_recv()
        pull(ga2.owner(sign, 3), 0)
    for sign in (1, -1):
        ga2.opposite(sign).wait_recv()
    ga2.pending = False
    pull(ga2.owner(1, 4), 0)

    to_x.recv()
    gy[y] = summed(gx_rec)
    over_y = Exchange(lambda d: remote(gy.at[y], gy.at[y], s_gy.at[d], r_gy.at[d], along("y", d)))
    over_y.start()

    gb2.recv()
    lax.fori_loop(0, RING, lambda at_x, carry: (pull(at_x, 256), carry)[1], 0)
    back[...] = acc[...].astype(BF).reshape(RING, 64, HALF)
    sums = Exchange(
        lambda d: remote(back.at[wrap(z + d)], rec_z.at[d], s_z.at[d], r_z.at[d], along("z", d))
    )
    sums.start()
    rec_z[0] = back[z]

    over_y.recv()
    total_y = summed(gy)
    gz[x] = total_y[:8]
    gbias[k] = total_y[8:]
    from_x = Exchange(lambda d: remote(gz.at[x], gz.at[x], s_hx.at[d], r_hx.at[d], along("x", d)))
    from_x.start()
    bias_swap = single(remote(gbias.at[k], gbias.at[k], s_hs.at[1], r_hs.at[1], at(x, y, z, sib)))
    bias_swap.start()

    sums.recv()
    b_own[...] = summed(rec_z).astype(BF).reshape(2, CHUNK, HALF)
    b_swap = single(remote(b_own.at[sib], b_sib, s_sib.at[0], r_sib.at[0], at(x, y, z, sib)))
    b_swap.start()

    from_x.recv()
    gfull[k, z] = gz[...].reshape(64, HALF).astype(BF)
    from_z = Exchange(
        lambda d: remote(gfull.at[k, z], gfull.at[k, z], s_hz.at[d], r_hz.at[d], along("z", d))
    )
    from_z.start()

    give_back.recv()
    act_out[:, pl.ds(0, HALF)] = act_ret[0]
    act_out[:, pl.ds(HALF, HALF)] = act_ret[1]
    own_part = dot_last(g_ret[0], w_self[:, pl.ds(0, HALF)]) + dot_last(
        g_ret[1], w_self[:, pl.ds(HALF, HALF)]
    )
    b_swap.recv()
    returned = dot_last(b_own[k], w_neigh[:, lanes]) + dot_last(
        b_sib[...], w_neigh[:, pl.ds(pl.multiple_of(HALF * sib, HALF), HALF)]
    )
    gf_out[...] = (own_part + returned * norm_factor).astype(BF)

    from_z.recv()
    full_swap = single(remote(gfull.at[k], gfull.at[k], s_hs.at[0], r_hs.at[0], at(x, y, z, sib)))
    full_swap.start()
    bias_swap.recv()
    for core in (0, 1):
        gb_out[:, pl.ds(HALF * core, HALF)] = gbias[core, pl.ds(0, 1), :] * grad_factor
    full_swap.recv()
    for core in (0, 1):
        gs_out[:, pl.ds(HALF * core, HALF)] = (
            gfull[core, pl.ds(0, 4)].reshape(F, HALF).astype(F32) * grad_factor
        )
        gn_out[:, pl.ds(HALF * core, HALF)] = (
            gfull[core, pl.ds(4, 4)].reshape(F, HALF).astype(F32) * grad_factor
        )
    finish()


def place(*refs):
    copies = [
        pltpu.make_async_copy(refs[i], refs[5 + i], refs[10].at[i]) for i in range(5)
    ]
    for copy in copies:
        copy.start()
    for copy in copies:
        copy.wait()


def shards(
    features, w_self, w_neigh, bias_vector, cotangent, adj_values, src_slots, dst_slots, slot_counts
):
    block_rows = features.shape[0]
    replicas = lax.axis_size("rep")
    node_total = block_rows * lax.axis_size("row")
    slot_total = adj_values.shape[2]
    norm_factor = 1.0 / math.sqrt(slot_total * replicas / (block_rows // adj_values.shape[-1]))
    grad_factor = 1.0 / math.sqrt(node_total)

    def body(*refs):
        kernel(norm_factor, grad_factor, *refs)

    vmem = pl.BlockSpec(memory_space=pltpu.VMEM)
    hbm = pl.BlockSpec(memory_space=pltpu.HBM)
    smem = pl.BlockSpec(memory_space=pltpu.SMEM)
    dma = pltpu.SemaphoreType.DMA
    sems = [
        dma((12,)), dma((4,)), dma((4,)), dma((1,)), dma((1,)), dma((13,)), dma((9,)), dma((13,)),
        dma((14,)), dma((8,)), dma((8,)), dma((8,)), dma((8,)),
        dma((1,)), dma((1,)), dma((8,)), dma((8,)), dma((8,)), dma((8,)), dma((8,)), dma((8,)),
        dma((8,)), dma((8,)), dma((4,)), dma((4,)),
        dma((8,)), dma((8,)), dma((8,)), dma((8,)), dma((8,)), dma((8,)), dma((8,)), dma((8,)),
        dma((8,)), dma((8,)), dma((2,)), dma((2,)),
        dma((8,)), dma((8,)), dma((1,)), dma((1,)),
    ]
    scratch = [
        pltpu.VMEM((NB, F), BF),
        pltpu.VMEM((F, F), BF),
        pltpu.VMEM((F, F), BF),
        pltpu.VMEM((NB, F), BF),
        pltpu.VMEM((1, F), F32),
        pltpu.SMEM((1, 1, 64), jnp.int32),
        pltpu.SMEM((1, 1, 64), jnp.int32),
        pltpu.VMEM((64, TILE, TILE), BF),
        pltpu.VMEM((8, NB, NB), BF),
        pltpu.VMEM((2, 4, NB, HALF), BF),
        pltpu.VMEM((5, 256, HALF), BF),
        pltpu.VMEM((5, 2, 4, CHUNK, HALF), BF),
        pltpu.VMEM((8, CHUNK, HALF), BF),
        pltpu.VMEM((8, CHUNK, HALF), BF),
        pltpu.VMEM((8, CHUNK, HALF), BF),
        pltpu.VMEM((8, CHUNK, HALF), BF),
        pltpu.VMEM((2, 64, HALF), BF),
        pltpu.VMEM((2, 2, 256, HALF), BF),
        pltpu.VMEM((2, 256, HALF), BF),
        pltpu.VMEM((2, 2, 256, HALF), BF),
        pltpu.VMEM((2, 2, 4, CHUNK, HALF), BF),
        pltpu.VMEM((2, 4, CHUNK, HALF), BF),
        pltpu.VMEM((2, 2, 4, CHUNK, HALF), BF),
        pltpu.VMEM((2, CHUNK, F), BF),
        pltpu.VMEM((2, CHUNK, HALF), BF),
        pltpu.VMEM((2, CHUNK, HALF), BF),
        pltpu.VMEM((2, CHUNK, HALF), BF),
        pltpu.VMEM((2, CHUNK, HALF), BF),
        pltpu.VMEM((2, CHUNK, HALF), BF),
        pltpu.VMEM((8, NB, HALF), BF),
        pltpu.VMEM((NB, HALF), F32),
        pltpu.VMEM((8, 64, HALF), BF),
        pltpu.VMEM((8, 64, HALF), BF),
        pltpu.VMEM((CHUNK, HALF), BF),
        pltpu.VMEM((2, CHUNK, HALF), BF),
        pltpu.VMEM((8, 72, HALF), F32),
        pltpu.VMEM((8, 72, HALF), F32),
        pltpu.VMEM((8, 16, HALF), F32),
        pltpu.VMEM((8, 16, HALF), F32),
        pltpu.VMEM((8, 16, HALF), F32),
        pltpu.VMEM((8, 8, HALF), F32),
        pltpu.VMEM((2, 8, 64, HALF), BF),
        pltpu.VMEM((2, 8, HALF), F32),
    ]
    outs = pl.pallas_call(
        body,
        out_shape=(
            jax.ShapeDtypeStruct((CHUNK, F), BF),
            jax.ShapeDtypeStruct((CHUNK, F), BF),
            jax.ShapeDtypeStruct((F, F), F32),
            jax.ShapeDtypeStruct((F, F), F32),
            jax.ShapeDtypeStruct((1, F), F32),
        ),
        in_specs=[hbm] * 8 + [smem],
        out_specs=(vmem,) * 5,
        scratch_shapes=scratch + sems,
        compiler_params=pltpu.CompilerParams(
            collective_id=0, has_side_effects=True, vmem_limit_bytes=48 << 20
        ),
        cost_estimate=pl.CostEstimate(
            flops=1_500_000_000, bytes_accessed=8_000_000, transcendentals=20_000
        ),
        name="sage_layer",
    )(
        *(
            pltpu.with_memory_space_constraint(array, pltpu.HBM)
            for array in (
                features, w_self, w_neigh, bias_vector.reshape(1, -1), cotangent, adj_values,
                src_slots, dst_slots,
            )
        ),
        slot_counts,
    )
    act, gf, gs, gn, gb = pl.pallas_call(
        place,
        out_shape=tuple(jax.ShapeDtypeStruct(out.shape, out.dtype) for out in outs),
        in_specs=[vmem] * 5,
        out_specs=(hbm,) * 5,
        scratch_shapes=[dma((5,))],
        compiler_params=pltpu.CompilerParams(vmem_limit_bytes=4 << 20),
        name="place_results",
    )(*outs)
    return act, gf, gs, gn, gb.reshape(-1)


def solution(mesh):
    placed = (
        P("row", None),
        P(),
        P(),
        P(),
        P("row", None),
        P("row", "rep", None, None, None),
        P("row", "rep", None),
        P("row", "rep", None),
        P("row", "rep"),
    )
    return jax.shard_map(
        shards,
        mesh=mesh,
        in_specs=placed,
        out_specs=(P(("row", "rep"), None), P(("row", "rep"), None), P(), P(), P()),
        check_vma=False,
    )
```

```python
import math

import jax
import jax.numpy as jnp
from jax import lax
from jax.experimental import pallas as pl
from jax.experimental.pallas import tpu as pltpu
from jax.sharding import PartitionSpec as P

RING = 8
HALF = 128
CHUNK = 32
TILE = 128
NB = 512
F = 256
MESH = pl.DeviceIdType.MESH
BF = jnp.bfloat16
F32 = jnp.float32


def wrap(value):
    return lax.rem(value, RING)


def dot_first(a, b):
    return lax.dot_general(a, b, (((0,), (0,)), ((), ())), preferred_element_type=F32)


def dot_last(a, b):
    return lax.dot_general(a, b, (((1,), (1,)), ((), ())), preferred_element_type=F32)


def kernel(
    norm_factor, grad_factor,
    feat_hbm, ws_hbm, wn_hbm, bias_hbm, cot_hbm, adj, src_hbm, dst_hbm, counts,
    act_out, gf_out, gs_out, gn_out, gb_out,
    feat, w_self, w_neigh, cot, bias, src_slots, dst_slots,
    tiles, dense, part, rec_a, rec_b, mid_a, mid_b, rec_a2, rec_b2, agg,
    rel_a3, rel_a4, comb_a, rel_b3, rel_b4, comb_b,
    f_rows, c_rows, g_own, a_own, act_ret, g_ret, gbuf, acc, back, rec_z, b_sib, b_own,
    gp, gp_rec, hx1, hy1, hy2, hx2, gfull, gbias,
    load_sem, s_t, r_t, s_adj, r_adj, s_a1, r_a1, s_b1, r_b1, s_a2, r_a2, s_b2, r_b2,
    s_agg, r_agg, s_ga1, r_ga1, s_gb1, r_gb1, s_ga2, r_ga2, s_gb2, r_gb2, s_ret, r_ret,
    s_gz, r_gz, s_gx, r_gx, s_gy, r_gy, s_hx, r_hx, s_hz, r_hz, s_hs, r_hs,
    s_z, r_z, s_sib, r_sib, s_hy, r_hy,
):
    row = lax.axis_index("row")
    rep = lax.axis_index("rep")
    y, x = row // RING, lax.rem(row, RING)
    z, k = rep // 2, lax.rem(rep, 2)
    sib = 1 - k

    def at(xx, yy, zz, kk):
        return (yy * RING + xx, zz * 2 + kk)

    def along(axis, d):
        if axis == "x":
            return at(wrap(x + d), y, z, k)
        if axis == "y":
            return at(x, wrap(y + d), z, k)
        return at(x, y, wrap(z + d), k)

    def remote(src, dst, send_sem, recv_sem, device):
        return pltpu.make_async_remote_copy(
            src_ref=src, dst_ref=dst, send_sem=send_sem, recv_sem=recv_sem,
            device_id=device, device_id_type=MESH,
        )

    def peers(fn):
        def step(i, carry):
            fn(4 + (1 - 2 * lax.rem(i, 2)) * ((i + 1) // 2))
            return carry

        lax.fori_loop(0, RING - 1, step, 0)

    def unless(condition, fn):
        pl.when(jnp.logical_not(condition))(fn)

    sent = []

    class Exchange:
        def __init__(self, copy, start=None, recv=None, done=None):
            self.copy = copy
            self.start_all = start or (lambda: peers(lambda d: copy(d).start()))
            self.recv_all = recv or (lambda: peers(lambda d: copy(d).wait_recv()))
            self.done = done or (lambda: peers(lambda d: copy(d).wait_send()))
            self.pending = False

        def start(self):
            self.start_all()
            self.begun()

        def begun(self):
            self.pending = True
            sent.append(self)

        def recv(self):
            self.recv_all()
            self.pending = False

    def single(copy):
        return Exchange(None, copy.start, copy.wait_recv, copy.wait_send)

    def finish():
        for exchange in sent:
            if exchange.pending:
                exchange.recv()
        for exchange in sent:
            exchange.done()

    own_chunk = rep
    worker_y = wrap(own_chunk)
    own_half = own_chunk // RING
    is_self = jnp.logical_and(worker_y == y, y == z)

    def worker(core):
        return at(x, worker_y, y, core)

    def owner(half):
        return at(x, z, 4 * half + y // 2, lax.rem(y, 2))

    def owner_is_self(half):
        return jnp.logical_and(is_self, own_half == half)

    def worker_is_self(core):
        return jnp.logical_and(is_self, k == core)

    load_tiles = [
        pltpu.make_async_copy(
            adj.at[0, 0, pl.ds(16 * part_no, 16)], tiles.at[pl.ds(16 * part_no, 16)],
            load_sem.at[5 + part_no],
        )
        for part_no in range(4)
    ]
    load_feat = pltpu.make_async_copy(feat_hbm, feat, load_sem.at[1])
    load_cot = pltpu.make_async_copy(cot_hbm, cot, load_sem.at[2])
    load_ws = pltpu.make_async_copy(ws_hbm, w_self, load_sem.at[3])
    load_wn = pltpu.make_async_copy(wn_hbm, w_neigh, load_sem.at[4])
    load_bias = pltpu.make_async_copy(bias_hbm, bias, load_sem.at[9])
    load_src = pltpu.make_async_copy(src_hbm, src_slots, load_sem.at[10])
    load_dst = pltpu.make_async_copy(dst_hbm, dst_slots, load_sem.at[11])
    for load in (
        load_src, load_dst, load_feat, *load_tiles, load_cot, load_ws, load_wn, load_bias
    ):
        load.start()

    barrier = pltpu.get_barrier_semaphore()

    def greet(device):
        pl.semaphore_signal(barrier, inc=1, device_id=device, device_id_type=MESH)

    def greet_peers(d):
        for axis in ("x", "y", "z"):
            greet(along(axis, d))

    peers(greet_peers)
    for d in (1, 2, RING - 2, RING - 1):
        greet(at(wrap(x + d), y, z, sib))
        greet(at(x, wrap(y + d), z, sib))
    greet(at(x, y, z, sib))
    for core in (0, 1):
        unless(worker_is_self(core), lambda core=core: greet(worker(core)))
        unless(owner_is_self(core), lambda core=core: greet(owner(core)))

    for load in (load_src, load_dst, load_feat, *load_tiles):
        load.wait()

    live = counts[0, 0]

    def build(section, pointer):
        for t in range(4):
            for u in range(4):
                slot = jnp.minimum(pointer, 63)
                hit = jnp.logical_and(
                    pointer < live,
                    jnp.logical_and(
                        src_slots[0, 0, slot] == section * 4 + u, dst_slots[0, 0, slot] == t
                    ),
                )
                tile = tiles[slot]
                dense[4 * k + section, pl.ds(t * TILE, TILE), pl.ds(u * TILE, TILE)] = jnp.where(
                    hit, tile, jnp.zeros_like(tile)
                )
                pointer = pointer + hit.astype(jnp.int32)
        return pointer

    def push(section, first):
        rows = pl.ds(first, 256)
        product = dot_first(dense[4 * k + section, :, rows], feat[...]).astype(BF)
        part[0, section, rows] = product[:, :HALF]
        part[1, section, rows] = product[:, HALF:]

    pointer = jnp.int32(0)
    for section in range(4):
        pointer = build(section, pointer)
        push(section, 256)
    for load in (load_cot, load_ws, load_wn, load_bias):
        load.wait()

    pl.semaphore_wait(barrier, 34 - 2 * is_self.astype(jnp.int32))

    mine_here = (x // 4) == k

    class Reduce:
        def __init__(self, axis, term, here, slot, rel3, rel4, comb, send_sem, recv_sem, width):
            self.axis, self.term, self.here, self.slot = axis, term, here, slot
            self.rel3, self.rel4, self.comb = rel3, rel4, comb
            self.send_sem, self.recv_sem, self.width = send_sem, recv_sem, width
            self.pending = False

        def to(self, d, core):
            if self.axis == "x":
                return at(wrap(x + d), y, z, core)
            return at(x, wrap(y + d), z, core)

        def slot_sem(self, number, core):
            return self.recv_sem.at[4 + number * self.width + (core if self.width == 2 else 0)]

        def copies(self, d):
            send, recv = self.send_sem, self.recv_sem
            if d == 4:
                return [
                    remote(
                        self.term(4).at[way], self.rel4.at[way], send.at[way], recv.at[way],
                        self.to(6 if way else 2, k),
                    )
                    for way in (0, 1)
                ]
            if d in (3, 5):
                way = 0 if d == 3 else 1
                return [
                    remote(
                        self.term(d), self.rel3.at[way], send.at[2 + way], recv.at[2 + way],
                        self.to(7 if way else 1, k),
                    )
                ]
            if d == 0:
                return [
                    remote(
                        self.term(0).at[sib], self.slot(0, k), send.at[12], self.slot_sem(0, k),
                        self.to(0, sib),
                    )
                ]
            number = {1: 1, 7: 2, 2: 3, 6: 4}[d]
            source = self.term(d) if number < 3 else self.comb.at[number - 3]
            return [
                remote(
                    source.at[lane], self.slot(number, k), send.at[2 + 2 * number + lane],
                    self.slot_sem(number, k), self.to(d, lane),
                )
                for lane in (0, 1)
            ]

        def when_here(self, d, fn):
            condition = self.here(d)
            if condition is None:
                fn()
            else:
                pl.when(condition)(fn)

        def each(self, method, *distances):
            def step(d):
                for copy in self.copies(d):
                    getattr(copy, method)()

            for d in distances:
                self.when_here(d, lambda d=d: step(d))

        def start(self):
            self.each("start", 4, 3, 5, 1, 7, 0)
            self.pending = True
            sent.append(self)

        def pass_on(self):
            def step(way, d):
                own, rel3, rel4 = self.term(d), self.rel3.at[way], self.rel4.at[way]
                remote(rel4, rel4, self.send_sem.at[0], self.recv_sem.at[way], self.to(0, sib)).wait_recv()
                remote(
                    rel3, rel3, self.send_sem.at[0], self.recv_sem.at[2 + way], self.to(0, sib)
                ).wait_recv()
                for lane in (0, 1):
                    total = own[lane].astype(F32) + rel3[lane].astype(F32)
                    if lane == way:
                        total = total + rel4[...].astype(F32)
                    self.comb[way, lane] = total.astype(BF)
                for copy in self.copies(d):
                    copy.start()

            for way, d in ((0, 2), (1, 6)):
                self.when_here(d, lambda way=way, d=d: step(way, d))

        def wait_slot(self, number, core):
            place = self.slot(number, core)
            remote(
                place, place, self.send_sem.at[0], self.slot_sem(number, core), self.to(0, sib)
            ).wait_recv()

        def recv(self):
            if self.width == 2:
                self.wait_slot(0, sib)
            else:
                unless(mine_here, lambda: self.wait_slot(0, 0))
            for number in (1, 2, 3, 4):
                for core in range(self.width):
                    self.wait_slot(number, core)
            self.pending = False

        def done(self):
            self.each("wait_send", *range(RING))

    def term_a(d):
        return part.at[:, lax.rem(x + d, 4), pl.ds(0, 256)]

    def term_b(d):
        return part.at[:, :, pl.ds(pl.multiple_of(256 + CHUNK * wrap(y + d), CHUNK), CHUNK)]

    a1 = Reduce(
        "x", term_a, lambda d: (wrap(x + d) // 4) == k, lambda number, core: rec_a.at[number],
        rel_a3, rel_a4, comb_a, s_a1, r_a1, 1,
    )
    b1 = Reduce(
        "y", term_b, lambda d: None, lambda number, core: rec_b.at[number, core],
        rel_b3, rel_b4, comb_b, s_b1, r_b1, 2,
    )
    b1.start()
    for section in range(4):
        push(section, 0)
    a1.start()
    rec_b[0, k] = part[k, :, pl.ds(pl.multiple_of(256 + CHUNK * y, CHUNK), CHUNK), :]

    @pl.when(mine_here)
    def _():
        rec_a[0] = part[k, x - 4 * k, pl.ds(0, 256), :]

    def t_copies(core):
        rows = pl.ds(CHUNK * own_chunk, CHUNK)
        return (
            remote(feat.at[rows], f_rows.at[own_half], s_t.at[core], r_t.at[own_half], worker(core)),
            remote(
                cot.at[rows, pl.ds(HALF * core, HALF)], c_rows.at[own_half],
                s_t.at[2 + core], r_t.at[2 + own_half], worker(core),
            ),
        )

    def t_each(method):
        def step(core):
            for copy in t_copies(core):
                getattr(copy, method)()

        for core in (0, 1):
            unless(worker_is_self(core), lambda core=core: step(core))

    def t_recv():
        def step(half):
            remote(f_rows.at[half], f_rows.at[half], s_t.at[0], r_t.at[half], owner(half)).wait_recv()
            remote(
                c_rows.at[half], c_rows.at[half], s_t.at[2], r_t.at[2 + half], owner(half)
            ).wait_recv()

        for half in (0, 1):
            unless(owner_is_self(half), lambda half=half: step(half))

    fetch = Exchange(None, lambda: t_each("start"), t_recv, lambda: t_each("wait_send"))
    fetch.start()

    @pl.when(is_self)
    def _():
        rows = pl.ds(pl.multiple_of(CHUNK * own_chunk, CHUNK), CHUNK)
        f_rows[own_half] = feat[rows, :]
        c_rows[own_half] = cot[rows, pl.ds(pl.multiple_of(HALF * k, HALF), HALF)]

    adj_swap = single(
        remote(
            dense.at[pl.ds(4 * k, 4)], dense.at[pl.ds(4 * k, 4)], s_adj.at[0], r_adj.at[0],
            at(x, y, z, sib),
        )
    )
    adj_swap.start()
    a1.pass_on()
    b1.pass_on()

    fetch.recv()
    lanes = pl.ds(pl.multiple_of(HALF * k, HALF), HALF)
    rows64 = f_rows[...].reshape(64, F)
    self_part = jnp.dot(rows64, w_self[:, lanes], preferred_element_type=F32) + bias[:, lanes]

    def summed(ref):
        total = ref[0].astype(F32)
        for d in range(1, ref.shape[0]):
            total = total + ref[d].astype(F32)
        return total

    a1.recv()
    mid_a[...] = summed(rec_a).astype(BF).reshape(RING, CHUNK, HALF)
    a2 = Exchange(
        lambda d: remote(
            mid_a.at[wrap(y + d)], rec_a2.at[d], s_a2.at[d], r_a2.at[d], along("y", d)
        )
    )
    a2.start()
    rec_a2[0] = mid_a[y]

    b1.recv()
    mid_b[...] = summed(rec_b).astype(BF).reshape(RING, CHUNK, HALF)
    b2 = Exchange(
        lambda d: remote(
            mid_b.at[wrap(x + d)], rec_b2.at[d], s_b2.at[d], r_b2.at[d], along("x", d)
        )
    )
    b2.start()
    rec_b2[0] = mid_b[x]

    a2.recv()
    agg[k, pl.ds(0, CHUNK), :] = (summed(rec_a2) * norm_factor).astype(BF)
    b2.recv()
    agg[k, pl.ds(CHUNK, CHUNK), :] = (summed(rec_b2) * norm_factor).astype(BF)
    agg_swap = single(remote(agg.at[k], agg.at[k], s_agg.at[0], r_agg.at[0], at(x, y, z, sib)))
    agg_swap.start()
    agg_swap.recv()

    pre = (
        self_part
        + jnp.dot(agg[0], w_neigh[pl.ds(0, HALF), lanes], preferred_element_type=F32)
        + jnp.dot(agg[1], w_neigh[pl.ds(HALF, HALF), lanes], preferred_element_type=F32)
    )
    low = jnp.exp(jnp.minimum(pre, 0.0))
    grad = (c_rows[...].reshape(64, HALF).astype(F32) * low).astype(BF)
    g_own[...] = grad.reshape(2, CHUNK, HALF)

    place_a = gbuf.at[x, pl.ds(CHUNK * y, CHUNK)]
    place_b = gbuf.at[x, pl.ds(256 + CHUNK * y, CHUNK)]
    ga1 = Exchange(
        lambda d: remote(g_own.at[0], place_a, s_ga1.at[d], r_ga1.at[d], along("y", d))
    )
    gb1 = Exchange(
        lambda d: remote(g_own.at[1], place_b, s_gb1.at[d], r_gb1.at[d], along("x", d))
    )
    ga1.start()
    gb1.start()
    gbuf[x, pl.ds(pl.multiple_of(CHUNK * y, CHUNK), CHUNK), :] = g_own[0]
    gbuf[x, pl.ds(pl.multiple_of(256 + CHUNK * y, CHUNK), CHUNK), :] = g_own[1]
    a_own[...] = jnp.where(pre > 0, pre, low - 1.0).astype(BF).reshape(2, CHUNK, HALF)

    def ret_copies(half):
        return (
            remote(a_own.at[half], act_ret.at[k], s_ret.at[half], r_ret.at[k], owner(half)),
            remote(g_own.at[half], g_ret.at[k], s_ret.at[2 + half], r_ret.at[2 + k], owner(half)),
        )

    def ret_each(method):
        def step(half):
            for copy in ret_copies(half):
                getattr(copy, method)()

        for half in (0, 1):
            unless(owner_is_self(half), lambda half=half: step(half))

    def ret_recv():
        def step(core):
            remote(
                act_ret.at[core], act_ret.at[core], s_ret.at[0], r_ret.at[core], worker(core)
            ).wait_recv()
            remote(
                g_ret.at[core], g_ret.at[core], s_ret.at[2], r_ret.at[2 + core], worker(core)
            ).wait_recv()

        for core in (0, 1):
            unless(worker_is_self(core), lambda core=core: step(core))

    give_back = Exchange(None, lambda: ret_each("start"), ret_recv, lambda: ret_each("wait_send"))
    give_back.start()

    @pl.when(is_self)
    def _():
        act_ret[k] = a_own[own_half]
        g_ret[k] = g_own[own_half]

    grad_s = dot_first(rows64, grad)
    grad_n = jnp.concatenate([dot_first(agg[0], grad), dot_first(agg[1], grad)], 0)
    terms = jnp.concatenate([grad_s, grad_n], 0).reshape(RING, 64, HALF)
    gp[:, pl.ds(0, 64), :] = terms.astype(BF)
    col_sum = jnp.broadcast_to(jnp.sum(grad.astype(F32), axis=0, keepdims=True), (16, HALF))
    gp[:, pl.ds(64, 16), :] = jnp.broadcast_to(col_sum[None], (RING, 16, HALF)).astype(BF)
    to_z = Exchange(
        lambda d: remote(gp.at[wrap(z + d)], gp_rec.at[z], s_gz.at[d], r_gz.at[d], along("z", d))
    )
    to_z.start()
    gp_rec[z] = gp[z]

    class Relay:
        def __init__(self, axis, me, piece, half, send_sem, recv_sem):
            self.axis, self.me, self.piece, self.half = axis, me, piece, half
            self.sems = (send_sem, recv_sem)
            self.pending = False
            self.done_all = []

        def copy(self, ref, sign, hop, tag):
            send_sem, recv_sem = self.sems
            index = 2 * tag + (sign < 0)
            return remote(
                ref, ref, send_sem.at[index], recv_sem.at[index],
                along(self.axis, (sign * hop) % RING),
            )

        def owner(self, sign, distance):
            return wrap(self.me + (-sign * distance) % RING)

        def near(self, sign):
            return self.copy(self.piece(self.me), sign, 1, 0)

        def next_near(self, sign):
            return self.copy(self.piece(self.me), sign, 2, 1)

        def far(self, sign):
            return self.copy(self.piece(self.owner(sign, 2)), sign, 1, 2)

        def opposite(self, sign):
            return self.copy(self.half(self.owner(sign, 2), sign), sign, 2, 3)

        def start(self):
            for sign in (1, -1):
                self.next_near(sign).start()
            for sign in (1, -1):
                self.near(sign).start()
            self.pending = True
            sent.append(self)

        def pass_on(self):
            for sign in (1, -1):
                self.next_near(sign).wait_recv()
                self.opposite(sign).start()
                self.far(sign).start()

        def recv(self):
            for sign in (1, -1):
                self.near(sign).wait_recv()
                self.far(sign).wait_recv()
                self.opposite(sign).wait_recv()
            self.pending = False

        def done(self):
            for sign in (1, -1):
                for copy in (self.near, self.next_near, self.far, self.opposite):
                    copy(sign).wait_send()

    ga2 = Relay(
        "x", x, lambda at_x: gbuf.at[at_x, pl.ds(0, 256)],
        lambda at_x, sign: gbuf.at[at_x, pl.ds(0 if sign > 0 else 128, 128)], s_ga2, r_ga2,
    )
    gb2 = Relay(
        "y", y, lambda at_y: gbuf.at[:, pl.ds(256 + CHUNK * at_y, CHUNK)],
        lambda at_y, sign: gbuf.at[
            pl.ds(0 if sign > 0 else 4, 4), pl.ds(256 + CHUNK * at_y, CHUNK)
        ], s_gb2, r_gb2,
    )
    ga1.recv()
    ga2.start()
    gb1.recv()
    gb2.start()

    to_z.recv()
    over_z = summed(gp_rec).astype(BF)
    hx1[x, pl.ds(0, 32), :] = over_z[:32]
    hx1[x, pl.ds(32, 16), :] = over_z[64:]
    hy2[y] = over_z[32:64]
    over_x1 = Exchange(lambda d: remote(hx1.at[x], hx1.at[x], s_gx.at[d], r_gx.at[d], along("x", d)))
    over_y2 = Exchange(lambda d: remote(hy2.at[y], hy2.at[y], s_hy.at[d], r_hy.at[d], along("y", d)))
    over_x1.start()
    over_y2.start()
    ga2.pass_on()
    gb2.pass_on()

    adj_swap.recv()

    def pull(at_x, first):
        acc[...] += jnp.dot(
            dense[at_x, :, pl.ds(first, 256)], gbuf[at_x, pl.ds(first, 256), :],
            preferred_element_type=F32,
        )

    acc[...] = jnp.zeros_like(acc)
    pull(x, 0)

    for sign in (1, -1):
        pull(ga2.owner(sign, 2), 0)
    for sign in (1, -1):
        ga2.near(sign).wait_recv()
        pull(ga2.owner(sign, 1), 0)

    over_x1.recv()
    hy1[y] = summed(hx1).astype(BF)
    over_y1 = Exchange(lambda d: remote(hy1.at[y], hy1.at[y], s_gy.at[d], r_gy.at[d], along("y", d)))
    over_y1.start()
    over_y2.recv()
    hx2[x] = summed(hy2).astype(BF)
    over_x2 = Exchange(lambda d: remote(hx2.at[x], hx2.at[x], s_hx.at[d], r_hx.at[d], along("x", d)))
    over_x2.start()

    for sign in (1, -1):
        ga2.far(sign).wait_recv()
        pull(ga2.owner(sign, 3), 0)
    for sign in (1, -1):
        ga2.opposite(sign).wait_recv()
    ga2.pending = False
    pull(ga2.owner(1, 4), 0)

    gb2.recv()
    lax.fori_loop(0, RING, lambda at_x, carry: (pull(at_x, 256), carry)[1], 0)
    back[...] = acc[...].astype(BF).reshape(RING, 64, HALF)
    sums = Exchange(
        lambda d: remote(back.at[wrap(z + d)], rec_z.at[d], s_z.at[d], r_z.at[d], along("z", d))
    )
    sums.start()
    rec_z[0] = back[z]

    over_y1.recv()
    total_1 = summed(hy1)
    over_x2.recv()
    total_2 = summed(hx2)
    gfull[k, z, pl.ds(0, 32), :] = total_1[:32].astype(BF)
    gfull[k, z, pl.ds(32, 32), :] = total_2.astype(BF)
    gbias[k] = total_1[32:40]
    from_z = Exchange(
        lambda d: remote(gfull.at[k, z], gfull.at[k, z], s_hz.at[d], r_hz.at[d], along("z", d))
    )
    from_z.start()
    bias_swap = single(remote(gbias.at[k], gbias.at[k], s_hs.at[1], r_hs.at[1], at(x, y, z, sib)))
    bias_swap.start()

    sums.recv()
    b_own[...] = summed(rec_z).astype(BF).reshape(2, CHUNK, HALF)
    b_swap = single(remote(b_own.at[sib], b_sib, s_sib.at[0], r_sib.at[0], at(x, y, z, sib)))
    b_swap.start()


    give_back.recv()
    act_out[:, pl.ds(0, HALF)] = act_ret[0]
    act_out[:, pl.ds(HALF, HALF)] = act_ret[1]
    own_part = dot_last(g_ret[0], w_self[:, pl.ds(0, HALF)]) + dot_last(
        g_ret[1], w_self[:, pl.ds(HALF, HALF)]
    )
    b_swap.recv()
    returned = dot_last(b_own[k], w_neigh[:, lanes]) + dot_last(
        b_sib[...], w_neigh[:, pl.ds(pl.multiple_of(HALF * sib, HALF), HALF)]
    )
    gf_out[...] = (own_part + returned * norm_factor).astype(BF)

    from_z.recv()
    full_swap = single(remote(gfull.at[k], gfull.at[k], s_hs.at[0], r_hs.at[0], at(x, y, z, sib)))
    full_swap.start()
    bias_swap.recv()
    for core in (0, 1):
        gb_out[:, pl.ds(HALF * core, HALF)] = gbias[core, pl.ds(0, 1), :] * grad_factor
    full_swap.recv()
    for core in (0, 1):
        gs_out[:, pl.ds(HALF * core, HALF)] = (
            gfull[core, pl.ds(0, 4)].reshape(F, HALF).astype(F32) * grad_factor
        )
        gn_out[:, pl.ds(HALF * core, HALF)] = (
            gfull[core, pl.ds(4, 4)].reshape(F, HALF).astype(F32) * grad_factor
        )
    finish()


def place(*refs):
    copies = [
        pltpu.make_async_copy(refs[i], refs[5 + i], refs[10].at[i]) for i in range(5)
    ]
    for copy in copies:
        copy.start()
    for copy in copies:
        copy.wait()


def shards(
    features, w_self, w_neigh, bias_vector, cotangent, adj_values, src_slots, dst_slots, slot_counts
):
    block_rows = features.shape[0]
    replicas = lax.axis_size("rep")
    node_total = block_rows * lax.axis_size("row")
    slot_total = adj_values.shape[2]
    norm_factor = 1.0 / math.sqrt(slot_total * replicas / (block_rows // adj_values.shape[-1]))
    grad_factor = 1.0 / math.sqrt(node_total)

    def body(*refs):
        kernel(norm_factor, grad_factor, *refs)

    vmem = pl.BlockSpec(memory_space=pltpu.VMEM)
    hbm = pl.BlockSpec(memory_space=pltpu.HBM)
    smem = pl.BlockSpec(memory_space=pltpu.SMEM)
    dma = pltpu.SemaphoreType.DMA
    sems = [
        dma((12,)), dma((4,)), dma((4,)), dma((1,)), dma((1,)), dma((13,)), dma((9,)), dma((13,)),
        dma((14,)), dma((8,)), dma((8,)), dma((8,)), dma((8,)),
        dma((1,)), dma((1,)), dma((8,)), dma((8,)), dma((8,)), dma((8,)), dma((8,)), dma((8,)),
        dma((8,)), dma((8,)), dma((4,)), dma((4,)),
        dma((8,)), dma((8,)), dma((8,)), dma((8,)), dma((8,)), dma((8,)), dma((8,)), dma((8,)),
        dma((8,)), dma((8,)), dma((2,)), dma((2,)),
        dma((8,)), dma((8,)), dma((1,)), dma((1,)), dma((8,)), dma((8,)),
    ]
    scratch = [
        pltpu.VMEM((NB, F), BF),
        pltpu.VMEM((F, F), BF),
        pltpu.VMEM((F, F), BF),
        pltpu.VMEM((NB, F), BF),
        pltpu.VMEM((1, F), F32),
        pltpu.SMEM((1, 1, 64), jnp.int32),
        pltpu.SMEM((1, 1, 64), jnp.int32),
        pltpu.VMEM((64, TILE, TILE), BF),
        pltpu.VMEM((8, NB, NB), BF),
        pltpu.VMEM((2, 4, NB, HALF), BF),
        pltpu.VMEM((5, 256, HALF), BF),
        pltpu.VMEM((5, 2, 4, CHUNK, HALF), BF),
        pltpu.VMEM((8, CHUNK, HALF), BF),
        pltpu.VMEM((8, CHUNK, HALF), BF),
        pltpu.VMEM((8, CHUNK, HALF), BF),
        pltpu.VMEM((8, CHUNK, HALF), BF),
        pltpu.VMEM((2, 64, HALF), BF),
        pltpu.VMEM((2, 2, 256, HALF), BF),
        pltpu.VMEM((2, 256, HALF), BF),
        pltpu.VMEM((2, 2, 256, HALF), BF),
        pltpu.VMEM((2, 2, 4, CHUNK, HALF), BF),
        pltpu.VMEM((2, 4, CHUNK, HALF), BF),
        pltpu.VMEM((2, 2, 4, CHUNK, HALF), BF),
        pltpu.VMEM((2, CHUNK, F), BF),
        pltpu.VMEM((2, CHUNK, HALF), BF),
        pltpu.VMEM((2, CHUNK, HALF), BF),
        pltpu.VMEM((2, CHUNK, HALF), BF),
        pltpu.VMEM((2, CHUNK, HALF), BF),
        pltpu.VMEM((2, CHUNK, HALF), BF),
        pltpu.VMEM((8, NB, HALF), BF),
        pltpu.VMEM((NB, HALF), F32),
        pltpu.VMEM((8, 64, HALF), BF),
        pltpu.VMEM((8, 64, HALF), BF),
        pltpu.VMEM((CHUNK, HALF), BF),
        pltpu.VMEM((2, CHUNK, HALF), BF),
        pltpu.VMEM((8, 80, HALF), BF),
        pltpu.VMEM((8, 80, HALF), BF),
        pltpu.VMEM((8, 48, HALF), BF),
        pltpu.VMEM((8, 48, HALF), BF),
        pltpu.VMEM((8, 32, HALF), BF),
        pltpu.VMEM((8, 32, HALF), BF),
        pltpu.VMEM((2, 8, 64, HALF), BF),
        pltpu.VMEM((2, 8, HALF), F32),
    ]
    outs = pl.pallas_call(
        body,
        out_shape=(
            jax.ShapeDtypeStruct((CHUNK, F), BF),
            jax.ShapeDtypeStruct((CHUNK, F), BF),
            jax.ShapeDtypeStruct((F, F), F32),
            jax.ShapeDtypeStruct((F, F), F32),
            jax.ShapeDtypeStruct((1, F), F32),
        ),
        in_specs=[hbm] * 8 + [smem],
        out_specs=(vmem,) * 5,
        scratch_shapes=scratch + sems,
        compiler_params=pltpu.CompilerParams(
            collective_id=0, has_side_effects=True, vmem_limit_bytes=48 << 20
        ),
        cost_estimate=pl.CostEstimate(
            flops=1_500_000_000, bytes_accessed=8_000_000, transcendentals=20_000
        ),
        name="sage_layer",
    )(
        *(
            pltpu.with_memory_space_constraint(array, pltpu.HBM)
            for array in (
                features, w_self, w_neigh, bias_vector.reshape(1, -1), cotangent, adj_values,
                src_slots, dst_slots,
            )
        ),
        slot_counts,
    )
    act, gf, gs, gn, gb = pl.pallas_call(
        place,
        out_shape=tuple(jax.ShapeDtypeStruct(out.shape, out.dtype) for out in outs),
        in_specs=[vmem] * 5,
        out_specs=(hbm,) * 5,
        scratch_shapes=[dma((5,))],
        compiler_params=pltpu.CompilerParams(vmem_limit_bytes=4 << 20),
        name="place_results",
    )(*outs)
    return act, gf, gs, gn, gb.reshape(-1)


def solution(mesh):
    placed = (
        P("row", None),
        P(),
        P(),
        P(),
        P("row", None),
        P("row", "rep", None, None, None),
        P("row", "rep", None),
        P("row", "rep", None),
        P("row", "rep"),
    )
    return jax.shard_map(
        shards,
        mesh=mesh,
        in_specs=placed,
        out_specs=(P(("row", "rep"), None), P(("row", "rep"), None), P(), P(), P()),
        check_vma=False,
    )
```

```python
import math

import jax
import jax.numpy as jnp
from jax import lax
from jax.experimental import pallas as pl
from jax.experimental.pallas import tpu as pltpu
from jax.sharding import PartitionSpec as P

RING = 8
HALF = 128
CHUNK = 32
TILE = 128
NB = 512
F = 256
MESH = pl.DeviceIdType.MESH
BF = jnp.bfloat16
F32 = jnp.float32


def wrap(value):
    return lax.rem(value, RING)


def dot_first(a, b):
    return lax.dot_general(a, b, (((0,), (0,)), ((), ())), preferred_element_type=F32)


def dot_last(a, b):
    return lax.dot_general(a, b, (((1,), (1,)), ((), ())), preferred_element_type=F32)


def kernel(
    norm_factor, grad_factor,
    feat_hbm, ws_hbm, wn_hbm, bias_hbm, cot_hbm, adj, src_hbm, dst_hbm, counts,
    act_out, gf_out, gs_out, gn_out, gb_out,
    feat, w_self, w_neigh, cot, bias, src_slots, dst_slots,
    tiles, dense, part, rec_a, rec_b, mid_a, mid_b, rec_a2, rec_b2, agg,
    rel_a3, rel_a4, comb_a, rel_b3, rel_b4, comb_b,
    f_rows, c_rows, g_own, a_own, act_ret, g_ret, gbuf, acc, back, rec_z, b_sib, b_own,
    gp, gp_rec, hx1, hy1, hy2, hx2, gfull, gbias,
    load_sem, s_t, r_t, s_adj, r_adj, s_a1, r_a1, s_b1, r_b1, s_a2, r_a2, s_b2, r_b2,
    s_agg, r_agg, s_ga1, r_ga1, s_gb1, r_gb1, s_ga2, r_ga2, s_gb2, r_gb2, s_ret, r_ret,
    s_gz, r_gz, s_gx, r_gx, s_gy, r_gy, s_hx, r_hx, s_hz, r_hz, s_hs, r_hs,
    s_z, r_z, s_sib, r_sib, s_hy, r_hy,
):
    row = lax.axis_index("row")
    rep = lax.axis_index("rep")
    y, x = row // RING, lax.rem(row, RING)
    z, k = rep // 2, lax.rem(rep, 2)
    sib = 1 - k

    def at(xx, yy, zz, kk):
        return (yy * RING + xx, zz * 2 + kk)

    def along(axis, d):
        if axis == "x":
            return at(wrap(x + d), y, z, k)
        if axis == "y":
            return at(x, wrap(y + d), z, k)
        return at(x, y, wrap(z + d), k)

    def remote(src, dst, send_sem, recv_sem, device):
        return pltpu.make_async_remote_copy(
            src_ref=src, dst_ref=dst, send_sem=send_sem, recv_sem=recv_sem,
            device_id=device, device_id_type=MESH,
        )

    def peers(fn):
        def step(i, carry):
            fn(4 + (1 - 2 * lax.rem(i, 2)) * ((i + 1) // 2))
            return carry

        lax.fori_loop(0, RING - 1, step, 0)

    def unless(condition, fn):
        pl.when(jnp.logical_not(condition))(fn)

    sent = []
    settled = []

    class Exchange:
        def __init__(self, copy, start=None, recv=None, done=None):
            self.copy = copy
            self.start_all = start or (lambda: peers(lambda d: copy(d).start()))
            self.recv_all = recv or (lambda: peers(lambda d: copy(d).wait_recv()))
            self.done = done or (lambda: peers(lambda d: copy(d).wait_send()))
            self.pending = False

        def start(self):
            self.start_all()
            self.begun()

        def begun(self):
            self.pending = True
            sent.append(self)

        def recv(self):
            self.recv_all()
            self.pending = False

    def single(copy):
        return Exchange(None, copy.start, copy.wait_recv, copy.wait_send)

    def settle():
        for exchange in sent:
            if not exchange.pending and exchange not in settled:
                settled.append(exchange)
                exchange.done()

    def finish():
        for exchange in sent:
            if exchange.pending:
                exchange.recv()
        settle()

    own_chunk = rep
    worker_y = wrap(own_chunk)
    own_half = own_chunk // RING
    is_self = jnp.logical_and(worker_y == y, y == z)

    def worker(core):
        return at(x, worker_y, y, core)

    def owner(half):
        return at(x, z, 4 * half + y // 2, lax.rem(y, 2))

    def owner_is_self(half):
        return jnp.logical_and(is_self, own_half == half)

    def worker_is_self(core):
        return jnp.logical_and(is_self, k == core)

    load_tiles = [
        pltpu.make_async_copy(
            adj.at[0, 0, pl.ds(16 * part_no, 16)], tiles.at[pl.ds(16 * part_no, 16)],
            load_sem.at[5 + part_no],
        )
        for part_no in range(4)
    ]
    load_feat = pltpu.make_async_copy(feat_hbm, feat, load_sem.at[1])
    load_cot = pltpu.make_async_copy(cot_hbm, cot, load_sem.at[2])
    load_ws = pltpu.make_async_copy(ws_hbm, w_self, load_sem.at[3])
    load_wn = pltpu.make_async_copy(wn_hbm, w_neigh, load_sem.at[4])
    load_bias = pltpu.make_async_copy(bias_hbm, bias, load_sem.at[9])
    load_src = pltpu.make_async_copy(src_hbm, src_slots, load_sem.at[10])
    load_dst = pltpu.make_async_copy(dst_hbm, dst_slots, load_sem.at[11])
    for load in (
        load_src, load_dst, load_feat, *load_tiles, load_cot, load_ws, load_wn, load_bias
    ):
        load.start()

    barrier = pltpu.get_barrier_semaphore()

    def greet(device):
        pl.semaphore_signal(barrier, inc=1, device_id=device, device_id_type=MESH)

    def greet_peers(d):
        for axis in ("x", "y", "z"):
            greet(along(axis, d))

    peers(greet_peers)
    for d in (1, 2, RING - 2, RING - 1):
        greet(at(wrap(x + d), y, z, sib))
        greet(at(x, wrap(y + d), z, sib))
    greet(at(x, y, z, sib))
    for core in (0, 1):
        unless(worker_is_self(core), lambda core=core: greet(worker(core)))
        unless(owner_is_self(core), lambda core=core: greet(owner(core)))

    for load in (load_src, load_dst, load_feat, *load_tiles):
        load.wait()

    live = counts[0, 0]

    def build(section, pointer):
        for t in range(4):
            for u in range(4):
                slot = jnp.minimum(pointer, 63)
                hit = jnp.logical_and(
                    pointer < live,
                    jnp.logical_and(
                        src_slots[0, 0, slot] == section * 4 + u, dst_slots[0, 0, slot] == t
                    ),
                )
                tile = tiles[slot]
                dense[section, pl.ds(t * TILE, TILE), pl.ds(u * TILE, TILE)] = jnp.where(
                    hit, tile, jnp.zeros_like(tile)
                )
                pointer = pointer + hit.astype(jnp.int32)
        return pointer

    def push(section, first):
        rows = pl.ds(first, 256)
        product = dot_first(dense[section, :, rows], feat[...]).astype(BF)
        part[0, section, rows] = product[:, :HALF]
        part[1, section, rows] = product[:, HALF:]

    pointer = jnp.int32(0)
    for section in range(4):
        pointer = build(section, pointer)
        push(section, 256)
    for load in (load_cot, load_ws, load_wn, load_bias):
        load.wait()

    pl.semaphore_wait(barrier, 34 - 2 * is_self.astype(jnp.int32))

    mine_here = (x // 4) == k

    class Reduce:
        def __init__(self, axis, term, here, slot, rel3, rel4, comb, send_sem, recv_sem, width):
            self.axis, self.term, self.here, self.slot = axis, term, here, slot
            self.rel3, self.rel4, self.comb = rel3, rel4, comb
            self.send_sem, self.recv_sem, self.width = send_sem, recv_sem, width
            self.pending = False

        def to(self, d, core):
            if self.axis == "x":
                return at(wrap(x + d), y, z, core)
            return at(x, wrap(y + d), z, core)

        def slot_sem(self, number, core):
            return self.recv_sem.at[4 + number * self.width + (core if self.width == 2 else 0)]

        def copies(self, d):
            send, recv = self.send_sem, self.recv_sem
            if d == 4:
                return [
                    remote(
                        self.term(4).at[way], self.rel4.at[way], send.at[way], recv.at[way],
                        self.to(6 if way else 2, k),
                    )
                    for way in (0, 1)
                ]
            if d in (3, 5):
                way = 0 if d == 3 else 1
                return [
                    remote(
                        self.term(d), self.rel3.at[way], send.at[2 + way], recv.at[2 + way],
                        self.to(7 if way else 1, k),
                    )
                ]
            if d == 0:
                return [
                    remote(
                        self.term(0).at[sib], self.slot(0, k), send.at[12], self.slot_sem(0, k),
                        self.to(0, sib),
                    )
                ]
            number = {1: 1, 7: 2, 2: 3, 6: 4}[d]
            source = self.term(d) if number < 3 else self.comb.at[number - 3]
            return [
                remote(
                    source.at[lane], self.slot(number, k), send.at[2 + 2 * number + lane],
                    self.slot_sem(number, k), self.to(d, lane),
                )
                for lane in (0, 1)
            ]

        def when_here(self, d, fn):
            condition = self.here(d)
            if condition is None:
                fn()
            else:
                pl.when(condition)(fn)

        def each(self, method, *distances):
            def step(d):
                for copy in self.copies(d):
                    getattr(copy, method)()

            for d in distances:
                self.when_here(d, lambda d=d: step(d))

        def start(self):
            self.each("start", 4, 3, 5, 1, 7, 0)
            self.pending = True
            sent.append(self)

        def pass_on(self):
            def step(way, d):
                own, rel3, rel4 = self.term(d), self.rel3.at[way], self.rel4.at[way]
                remote(rel4, rel4, self.send_sem.at[0], self.recv_sem.at[way], self.to(0, sib)).wait_recv()
                remote(
                    rel3, rel3, self.send_sem.at[0], self.recv_sem.at[2 + way], self.to(0, sib)
                ).wait_recv()
                for lane in (0, 1):
                    total = own[lane].astype(F32) + rel3[lane].astype(F32)
                    if lane == way:
                        total = total + rel4[...].astype(F32)
                    self.comb[way, lane] = total.astype(BF)
                for copy in self.copies(d):
                    copy.start()

            for way, d in ((0, 2), (1, 6)):
                self.when_here(d, lambda way=way, d=d: step(way, d))

        def wait_slot(self, number, core):
            place = self.slot(number, core)
            remote(
                place, place, self.send_sem.at[0], self.slot_sem(number, core), self.to(0, sib)
            ).wait_recv()

        def recv(self):
            if self.width == 2:
                self.wait_slot(0, sib)
            else:
                unless(mine_here, lambda: self.wait_slot(0, 0))
            for number in (1, 2, 3, 4):
                for core in range(self.width):
                    self.wait_slot(number, core)
            self.pending = False

        def done(self):
            self.each("wait_send", *range(RING))

    def term_a(d):
        return part.at[:, lax.rem(x + d, 4), pl.ds(0, 256)]

    def term_b(d):
        return part.at[:, :, pl.ds(pl.multiple_of(256 + CHUNK * wrap(y + d), CHUNK), CHUNK)]

    a1 = Reduce(
        "x", term_a, lambda d: (wrap(x + d) // 4) == k, lambda number, core: rec_a.at[number],
        rel_a3, rel_a4, comb_a, s_a1, r_a1, 1,
    )
    b1 = Reduce(
        "y", term_b, lambda d: None, lambda number, core: rec_b.at[number, core],
        rel_b3, rel_b4, comb_b, s_b1, r_b1, 2,
    )
    b1.start()
    for section in range(4):
        push(section, 0)
    a1.start()
    rec_b[0, k] = part[k, :, pl.ds(pl.multiple_of(256 + CHUNK * y, CHUNK), CHUNK), :]

    @pl.when(mine_here)
    def _():
        rec_a[0] = part[k, x - 4 * k, pl.ds(0, 256), :]

    def t_copies(core):
        rows = pl.ds(CHUNK * own_chunk, CHUNK)
        return (
            remote(feat.at[rows], f_rows.at[own_half], s_t.at[core], r_t.at[own_half], worker(core)),
            remote(
                cot.at[rows, pl.ds(HALF * core, HALF)], c_rows.at[own_half],
                s_t.at[2 + core], r_t.at[2 + own_half], worker(core),
            ),
        )

    def t_each(method):
        def step(core):
            for copy in t_copies(core):
                getattr(copy, method)()

        for core in (0, 1):
            unless(worker_is_self(core), lambda core=core: step(core))

    def t_recv():
        def step(half):
            remote(f_rows.at[half], f_rows.at[half], s_t.at[0], r_t.at[half], owner(half)).wait_recv()
            remote(
                c_rows.at[half], c_rows.at[half], s_t.at[2], r_t.at[2 + half], owner(half)
            ).wait_recv()

        for half in (0, 1):
            unless(owner_is_self(half), lambda half=half: step(half))

    fetch = Exchange(None, lambda: t_each("start"), t_recv, lambda: t_each("wait_send"))
    fetch.start()

    @pl.when(is_self)
    def _():
        rows = pl.ds(pl.multiple_of(CHUNK * own_chunk, CHUNK), CHUNK)
        f_rows[own_half] = feat[rows, :]
        c_rows[own_half] = cot[rows, pl.ds(pl.multiple_of(HALF * k, HALF), HALF)]

    adj_swap = single(
        remote(
            dense.at[pl.ds(0, 4)], dense.at[pl.ds(4, 4)], s_adj.at[0], r_adj.at[0],
            at(x, y, z, sib),
        )
    )
    b1.pass_on()
    a1.pass_on()
    adj_swap.start()

    def summed(ref):
        total = ref[0].astype(F32)
        for d in range(1, ref.shape[0]):
            total = total + ref[d].astype(F32)
        return total

    b1.recv()
    mid_b[...] = summed(rec_b).astype(BF).reshape(RING, CHUNK, HALF)
    b2 = Exchange(
        lambda d: remote(
            mid_b.at[wrap(x + d)], rec_b2.at[d], s_b2.at[d], r_b2.at[d], along("x", d)
        )
    )
    b2.start()
    rec_b2[0] = mid_b[x]
    a1.recv()
    mid_a[...] = summed(rec_a).astype(BF).reshape(RING, CHUNK, HALF)
    a2 = Exchange(
        lambda d: remote(
            mid_a.at[wrap(y + d)], rec_a2.at[d], s_a2.at[d], r_a2.at[d], along("y", d)
        )
    )
    a2.start()
    rec_a2[0] = mid_a[y]

    fetch.recv()
    lanes = pl.ds(pl.multiple_of(HALF * k, HALF), HALF)
    rows64 = f_rows[...].reshape(64, F)
    self_part = jnp.dot(rows64, w_self[:, lanes], preferred_element_type=F32) + bias[:, lanes]

    a2.recv()
    agg[k, pl.ds(0, CHUNK), :] = (summed(rec_a2) * norm_factor).astype(BF)
    b2.recv()
    agg[k, pl.ds(CHUNK, CHUNK), :] = (summed(rec_b2) * norm_factor).astype(BF)
    agg_swap = single(remote(agg.at[k], agg.at[k], s_agg.at[0], r_agg.at[0], at(x, y, z, sib)))
    agg_swap.start()
    agg_swap.recv()

    pre = (
        self_part
        + jnp.dot(agg[0], w_neigh[pl.ds(0, HALF), lanes], preferred_element_type=F32)
        + jnp.dot(agg[1], w_neigh[pl.ds(HALF, HALF), lanes], preferred_element_type=F32)
    )
    low = jnp.exp(jnp.minimum(pre, 0.0))
    grad = (c_rows[...].reshape(64, HALF).astype(F32) * low).astype(BF)
    g_own[...] = grad.reshape(2, CHUNK, HALF)

    place_a = gbuf.at[x, pl.ds(CHUNK * y, CHUNK)]
    place_b = gbuf.at[x, pl.ds(256 + CHUNK * y, CHUNK)]
    ga1 = Exchange(
        lambda d: remote(g_own.at[0], place_a, s_ga1.at[d], r_ga1.at[d], along("y", d))
    )
    gb1 = Exchange(
        lambda d: remote(g_own.at[1], place_b, s_gb1.at[d], r_gb1.at[d], along("x", d))
    )
    ga1.start()
    gb1.start()
    gbuf[x, pl.ds(pl.multiple_of(CHUNK * y, CHUNK), CHUNK), :] = g_own[0]
    gbuf[x, pl.ds(pl.multiple_of(256 + CHUNK * y, CHUNK), CHUNK), :] = g_own[1]
    grad_s = dot_first(rows64, grad)
    grad_n = jnp.concatenate([dot_first(agg[0], grad), dot_first(agg[1], grad)], 0)
    terms = jnp.concatenate([grad_s, grad_n], 0).reshape(RING, 64, HALF)
    gp[:, pl.ds(0, 64), :] = terms.astype(BF)
    col_sum = jnp.broadcast_to(jnp.sum(grad.astype(F32), axis=0, keepdims=True), (16, HALF))
    gp[:, pl.ds(64, 16), :] = jnp.broadcast_to(col_sum[None], (RING, 16, HALF)).astype(BF)
    to_z = Exchange(
        lambda d: remote(gp.at[wrap(z + d)], gp_rec.at[z], s_gz.at[d], r_gz.at[d], along("z", d))
    )
    to_z.start()
    gp_rec[z] = gp[z]

    a_own[...] = jnp.where(pre > 0, pre, low - 1.0).astype(BF).reshape(2, CHUNK, HALF)

    def ret_copies(half):
        return (
            remote(a_own.at[half], act_ret.at[k], s_ret.at[half], r_ret.at[k], owner(half)),
            remote(g_own.at[half], g_ret.at[k], s_ret.at[2 + half], r_ret.at[2 + k], owner(half)),
        )

    def ret_each(method):
        def step(half):
            for copy in ret_copies(half):
                getattr(copy, method)()

        for half in (0, 1):
            unless(owner_is_self(half), lambda half=half: step(half))

    def ret_recv():
        def step(core):
            remote(
                act_ret.at[core], act_ret.at[core], s_ret.at[0], r_ret.at[core], worker(core)
            ).wait_recv()
            remote(
                g_ret.at[core], g_ret.at[core], s_ret.at[2], r_ret.at[2 + core], worker(core)
            ).wait_recv()

        for core in (0, 1):
            unless(worker_is_self(core), lambda core=core: step(core))

    give_back = Exchange(None, lambda: ret_each("start"), ret_recv, lambda: ret_each("wait_send"))
    give_back.start()

    @pl.when(is_self)
    def _():
        act_ret[k] = a_own[own_half]
        g_ret[k] = g_own[own_half]


    class Relay:
        def __init__(self, axis, me, piece, half, send_sem, recv_sem):
            self.axis, self.me, self.piece, self.half = axis, me, piece, half
            self.sems = (send_sem, recv_sem)
            self.pending = False
            self.done_all = []

        def copy(self, ref, sign, hop, tag):
            send_sem, recv_sem = self.sems
            index = 2 * tag + (sign < 0)
            return remote(
                ref, ref, send_sem.at[index], recv_sem.at[index],
                along(self.axis, (sign * hop) % RING),
            )

        def owner(self, sign, distance):
            return wrap(self.me + (-sign * distance) % RING)

        def near(self, sign):
            return self.copy(self.piece(self.me), sign, 1, 0)

        def next_near(self, sign):
            return self.copy(self.piece(self.me), sign, 2, 1)

        def far(self, sign):
            return self.copy(self.piece(self.owner(sign, 2)), sign, 1, 2)

        def opposite(self, sign):
            return self.copy(self.half(self.owner(sign, 2), sign), sign, 2, 3)

        def start(self):
            for sign in (1, -1):
                self.next_near(sign).start()
            for sign in (1, -1):
                self.near(sign).start()
            self.pending = True
            sent.append(self)

        def pass_on(self):
            for sign in (1, -1):
                self.next_near(sign).wait_recv()
                self.opposite(sign).start()
                self.far(sign).start()

        def recv(self):
            for sign in (1, -1):
                self.near(sign).wait_recv()
                self.far(sign).wait_recv()
                self.opposite(sign).wait_recv()
            self.pending = False

        def done(self):
            for sign in (1, -1):
                for copy in (self.near, self.next_near, self.far, self.opposite):
                    copy(sign).wait_send()

    ga2 = Relay(
        "x", x, lambda at_x: gbuf.at[at_x, pl.ds(0, 256)],
        lambda at_x, sign: gbuf.at[at_x, pl.ds(0 if sign > 0 else 128, 128)], s_ga2, r_ga2,
    )
    gb2 = Relay(
        "y", y, lambda at_y: gbuf.at[:, pl.ds(256 + CHUNK * at_y, CHUNK)],
        lambda at_y, sign: gbuf.at[
            pl.ds(0 if sign > 0 else 4, 4), pl.ds(256 + CHUNK * at_y, CHUNK)
        ], s_gb2, r_gb2,
    )
    settle()
    ga1.recv()
    ga2.start()
    gb1.recv()
    gb2.start()

    to_z.recv()
    over_z = summed(gp_rec).astype(BF)
    hx1[x, pl.ds(0, 32), :] = over_z[:32]
    hx1[x, pl.ds(32, 16), :] = over_z[64:]
    hy2[y] = over_z[32:64]
    over_x1 = Exchange(lambda d: remote(hx1.at[x], hx1.at[x], s_gx.at[d], r_gx.at[d], along("x", d)))
    over_y2 = Exchange(lambda d: remote(hy2.at[y], hy2.at[y], s_hy.at[d], r_hy.at[d], along("y", d)))
    over_x1.start()
    over_y2.start()
    ga2.pass_on()
    gb2.pass_on()

    adj_swap.recv()

    def strip(at_x):
        return lax.rem(at_x, 4) + 4 * lax.rem(at_x // 4 + k, 2)

    def pull(at_x, first):
        acc[...] += jnp.dot(
            dense[strip(at_x), :, pl.ds(first, 256)], gbuf[at_x, pl.ds(first, 256), :],
            preferred_element_type=F32,
        )

    acc[...] = jnp.zeros_like(acc)
    pull(x, 0)

    for sign in (1, -1):
        pull(ga2.owner(sign, 2), 0)
    for sign in (1, -1):
        ga2.near(sign).wait_recv()
        pull(ga2.owner(sign, 1), 0)

    over_x1.recv()
    hy1[y] = summed(hx1).astype(BF)
    over_y1 = Exchange(lambda d: remote(hy1.at[y], hy1.at[y], s_gy.at[d], r_gy.at[d], along("y", d)))
    over_y1.start()
    over_y2.recv()
    hx2[x] = summed(hy2).astype(BF)
    over_x2 = Exchange(lambda d: remote(hx2.at[x], hx2.at[x], s_hx.at[d], r_hx.at[d], along("x", d)))
    over_x2.start()

    for sign in (1, -1):
        ga2.far(sign).wait_recv()
        pull(ga2.owner(sign, 3), 0)
    for sign in (1, -1):
        ga2.opposite(sign).wait_recv()
    ga2.pending = False
    pull(ga2.owner(1, 4), 0)

    gb2.recv()
    lax.fori_loop(0, RING, lambda at_x, carry: (pull(at_x, 256), carry)[1], 0)
    back[...] = acc[...].astype(BF).reshape(RING, 64, HALF)
    sums = Exchange(
        lambda d: remote(back.at[wrap(z + d)], rec_z.at[d], s_z.at[d], r_z.at[d], along("z", d))
    )
    sums.start()
    rec_z[0] = back[z]

    settle()
    over_y1.recv()
    total_1 = summed(hy1)
    over_x2.recv()
    total_2 = summed(hx2)
    gfull[k, z, pl.ds(0, 32), :] = total_1[:32].astype(BF)
    gfull[k, z, pl.ds(32, 32), :] = total_2.astype(BF)
    gbias[k] = total_1[32:40]
    from_z = Exchange(
        lambda d: remote(gfull.at[k, z], gfull.at[k, z], s_hz.at[d], r_hz.at[d], along("z", d))
    )
    from_z.start()
    bias_swap = single(remote(gbias.at[k], gbias.at[k], s_hs.at[1], r_hs.at[1], at(x, y, z, sib)))
    bias_swap.start()

    sums.recv()
    b_own[...] = summed(rec_z).astype(BF).reshape(2, CHUNK, HALF)
    b_swap = single(remote(b_own.at[sib], b_sib, s_sib.at[0], r_sib.at[0], at(x, y, z, sib)))
    b_swap.start()


    give_back.recv()
    act_out[:, pl.ds(0, HALF)] = act_ret[0]
    act_out[:, pl.ds(HALF, HALF)] = act_ret[1]
    own_part = dot_last(g_ret[0], w_self[:, pl.ds(0, HALF)]) + dot_last(
        g_ret[1], w_self[:, pl.ds(HALF, HALF)]
    )
    b_swap.recv()
    returned = dot_last(b_own[k], w_neigh[:, lanes]) + dot_last(
        b_sib[...], w_neigh[:, pl.ds(pl.multiple_of(HALF * sib, HALF), HALF)]
    )
    gf_out[...] = (own_part + returned * norm_factor).astype(BF)

    settle()
    from_z.recv()
    full_swap = single(remote(gfull.at[k], gfull.at[k], s_hs.at[0], r_hs.at[0], at(x, y, z, sib)))
    full_swap.start()
    bias_swap.recv()
    for core in (0, 1):
        gb_out[:, pl.ds(HALF * core, HALF)] = gbias[core, pl.ds(0, 1), :] * grad_factor
    full_swap.recv()
    for core in (0, 1):
        gs_out[:, pl.ds(HALF * core, HALF)] = (
            gfull[core, pl.ds(0, 4)].reshape(F, HALF).astype(F32) * grad_factor
        )
        gn_out[:, pl.ds(HALF * core, HALF)] = (
            gfull[core, pl.ds(4, 4)].reshape(F, HALF).astype(F32) * grad_factor
        )
    finish()


def place(*refs):
    copies = [
        pltpu.make_async_copy(refs[i], refs[5 + i], refs[10].at[i]) for i in range(5)
    ]
    for copy in copies:
        copy.start()
    for copy in copies:
        copy.wait()


def shards(
    features, w_self, w_neigh, bias_vector, cotangent, adj_values, src_slots, dst_slots, slot_counts
):
    block_rows = features.shape[0]
    replicas = lax.axis_size("rep")
    node_total = block_rows * lax.axis_size("row")
    slot_total = adj_values.shape[2]
    norm_factor = 1.0 / math.sqrt(slot_total * replicas / (block_rows // adj_values.shape[-1]))
    grad_factor = 1.0 / math.sqrt(node_total)

    def body(*refs):
        kernel(norm_factor, grad_factor, *refs)

    vmem = pl.BlockSpec(memory_space=pltpu.VMEM)
    hbm = pl.BlockSpec(memory_space=pltpu.HBM)
    smem = pl.BlockSpec(memory_space=pltpu.SMEM)
    dma = pltpu.SemaphoreType.DMA
    sems = [
        dma((12,)), dma((4,)), dma((4,)), dma((1,)), dma((1,)), dma((13,)), dma((9,)), dma((13,)),
        dma((14,)), dma((8,)), dma((8,)), dma((8,)), dma((8,)),
        dma((1,)), dma((1,)), dma((8,)), dma((8,)), dma((8,)), dma((8,)), dma((8,)), dma((8,)),
        dma((8,)), dma((8,)), dma((4,)), dma((4,)),
        dma((8,)), dma((8,)), dma((8,)), dma((8,)), dma((8,)), dma((8,)), dma((8,)), dma((8,)),
        dma((8,)), dma((8,)), dma((2,)), dma((2,)),
        dma((8,)), dma((8,)), dma((1,)), dma((1,)), dma((8,)), dma((8,)),
    ]
    scratch = [
        pltpu.VMEM((NB, F), BF),
        pltpu.VMEM((F, F), BF),
        pltpu.VMEM((F, F), BF),
        pltpu.VMEM((NB, F), BF),
        pltpu.VMEM((1, F), F32),
        pltpu.SMEM((1, 1, 64), jnp.int32),
        pltpu.SMEM((1, 1, 64), jnp.int32),
        pltpu.VMEM((64, TILE, TILE), BF),
        pltpu.VMEM((8, NB, NB), BF),
        pltpu.VMEM((2, 4, NB, HALF), BF),
        pltpu.VMEM((5, 256, HALF), BF),
        pltpu.VMEM((5, 2, 4, CHUNK, HALF), BF),
        pltpu.VMEM((8, CHUNK, HALF), BF),
        pltpu.VMEM((8, CHUNK, HALF), BF),
        pltpu.VMEM((8, CHUNK, HALF), BF),
        pltpu.VMEM((8, CHUNK, HALF), BF),
        pltpu.VMEM((2, 64, HALF), BF),
        pltpu.VMEM((2, 2, 256, HALF), BF),
        pltpu.VMEM((2, 256, HALF), BF),
        pltpu.VMEM((2, 2, 256, HALF), BF),
        pltpu.VMEM((2, 2, 4, CHUNK, HALF), BF),
        pltpu.VMEM((2, 4, CHUNK, HALF), BF),
        pltpu.VMEM((2, 2, 4, CHUNK, HALF), BF),
        pltpu.VMEM((2, CHUNK, F), BF),
        pltpu.VMEM((2, CHUNK, HALF), BF),
        pltpu.VMEM((2, CHUNK, HALF), BF),
        pltpu.VMEM((2, CHUNK, HALF), BF),
        pltpu.VMEM((2, CHUNK, HALF), BF),
        pltpu.VMEM((2, CHUNK, HALF), BF),
        pltpu.VMEM((8, NB, HALF), BF),
        pltpu.VMEM((NB, HALF), F32),
        pltpu.VMEM((8, 64, HALF), BF),
        pltpu.VMEM((8, 64, HALF), BF),
        pltpu.VMEM((CHUNK, HALF), BF),
        pltpu.VMEM((2, CHUNK, HALF), BF),
        pltpu.VMEM((8, 80, HALF), BF),
        pltpu.VMEM((8, 80, HALF), BF),
        pltpu.VMEM((8, 48, HALF), BF),
        pltpu.VMEM((8, 48, HALF), BF),
        pltpu.VMEM((8, 32, HALF), BF),
        pltpu.VMEM((8, 32, HALF), BF),
        pltpu.VMEM((2, 8, 64, HALF), BF),
        pltpu.VMEM((2, 8, HALF), F32),
    ]
    outs = pl.pallas_call(
        body,
        out_shape=(
            jax.ShapeDtypeStruct((CHUNK, F), BF),
            jax.ShapeDtypeStruct((CHUNK, F), BF),
            jax.ShapeDtypeStruct((F, F), F32),
            jax.ShapeDtypeStruct((F, F), F32),
            jax.ShapeDtypeStruct((1, F), F32),
        ),
        in_specs=[hbm] * 8 + [smem],
        out_specs=(vmem,) * 5,
        scratch_shapes=scratch + sems,
        compiler_params=pltpu.CompilerParams(
            collective_id=0, has_side_effects=True, vmem_limit_bytes=48 << 20
        ),
        cost_estimate=pl.CostEstimate(
            flops=1_500_000_000, bytes_accessed=8_000_000, transcendentals=20_000
        ),
        name="sage_layer",
    )(
        *(
            pltpu.with_memory_space_constraint(array, pltpu.HBM)
            for array in (
                features, w_self, w_neigh, bias_vector.reshape(1, -1), cotangent, adj_values,
                src_slots, dst_slots,
            )
        ),
        slot_counts,
    )
    act, gf, gs, gn, gb = pl.pallas_call(
        place,
        out_shape=tuple(jax.ShapeDtypeStruct(out.shape, out.dtype) for out in outs),
        in_specs=[vmem] * 5,
        out_specs=(hbm,) * 5,
        scratch_shapes=[dma((5,))],
        compiler_params=pltpu.CompilerParams(vmem_limit_bytes=4 << 20),
        name="place_results",
    )(*outs)
    return act, gf, gs, gn, gb.reshape(-1)


def solution(mesh):
    placed = (
        P("row", None),
        P(),
        P(),
        P(),
        P("row", None),
        P("row", "rep", None, None, None),
        P("row", "rep", None),
        P("row", "rep", None),
        P("row", "rep"),
    )
    return jax.shard_map(
        shards,
        mesh=mesh,
        in_specs=placed,
        out_specs=(P(("row", "rep"), None), P(("row", "rep"), None), P(), P(), P()),
        check_vma=False,
    )
```
